32 devices in a mesh: rep: 4 (over y, x), shard: 8 (over z, core).
Axes of the slice: x: 2, y: 2, z: 4, core: 2. Of those that a mesh axis runs over, the one named last changes fastest.
Arguments:
- bag_ids: int32 [2048, 20], P(('rep', 'shard')), may hold values from 0 to 4095
- table: float32 [4096, 256], P('shard'), may hold values from -1.2 to 1.2
- accum: float32 [4096], P('shard'), may hold values from 0.01 to 0.1
- cross_weight: float32 [256, 256], replicated, may hold values from -0.375 to 0.375
- cross_bias: float32 [256], replicated, may hold values from -4 to 4
- upstream: float32 [2048, 256], P(('rep', 'shard')), may hold values from -6 to 6
Outputs:
- crossed: float32 [2048, 256], P(('rep', 'shard'))
- new_table: float32 [4096, 256], P('shard')
- new_accum: float32 [4096], P('shard')
The draws below stay inside these ranges and needn't reach their ends.
All inputs are finite; a program needn't handle non-finite values.
Results may differ from the reference program's by a relative error of at most 0.00014.
Values sent between devices are 32-bit elements; how exact they have to be, the bound alone decides.
A program may use at most 64 MiB of HBM per device.

```python
import math
import jax
import jax.numpy as jnp
import numpy as np
from jax import lax

E = 256
BAG = 20
ROWS = 4096
SAMPLES = 2048


def set_ends(array, own_key, smallest, high):
    longest = array.shape.index(max(array.shape))
    spots = []
    for shift in (0, 1):
        where = [jax.random.randint(jax.random.fold_in(own_key, axis), (), 0, length) for axis, length in enumerate(array.shape)]
        where[longest] = (where[longest] + shift) % array.shape[longest]
        spots.append(tuple(where))
    return array.at[spots[0]].set(smallest).at[spots[1]].set(high)


def block_scale(rng, extent, cuts, least, top_value):
    gain = 1.0
    for position, shards_of in cuts:
        steps = jax.random.uniform(jax.random.fold_in(jax.random.fold_in(rng, 6), position), (shards_of,), jnp.float32, least / len(cuts), top_value / len(cuts))
        gain = gain * jnp.repeat(jnp.exp(steps), extent[position] // shards_of).reshape((-1,) + (1,) * (len(extent) - 1 - position))
    return gain


def rank_bounds(count, lean):
    weights = [(1 << 20) // math.isqrt(standing ** lean) + 1 for standing in range(1, count + 1)]
    spread = 1 + sum(weights) // (1 << 30)
    return np.cumsum(np.array([max(1, weight // spread) for weight in weights]))


def ranked_ids(stream_key, shape, number_of, slope):
    grid = rank_bounds(number_of, slope)
    lot = jax.random.randint(jax.random.fold_in(stream_key, 1), shape, 0, int(grid[number_of - 1]))
    rank = jnp.searchsorted(jnp.asarray(grid, jnp.int32), lot, side="right")
    return jax.random.permutation(jax.random.fold_in(stream_key, 2), number_of)[rank].astype(jnp.int32)


def scatter_about(rng, shape, spread, reach, shards=(), kind=jnp.bfloat16):
    level = block_scale(rng, shape, shards, -0.22, 0.18) if shards else 1.0
    result = jax.random.normal(rng, shape, jnp.float32) * spread * level
    return jnp.minimum(jnp.maximum(result, -reach), reach).astype(kind)


def setup_inputs(seed: int = 0) -> dict:
    key_of = jax.random.split(jax.random.key(seed), 7)
    return {
        "bag_ids": set_ends(ranked_ids(key_of[0], (SAMPLES, BAG), ROWS, 2), jax.random.fold_in(key_of[0], 3), 0, ROWS - 1).astype(jnp.int32),
        "table": scatter_about(key_of[1], (ROWS, E), 0.2, 1.2, ((0, 8),), jnp.float32),
        "accum": jnp.clip(jnp.exp(math.log(0.1) - 2.3025851 * jax.random.uniform(key_of[2], (ROWS,), jnp.float32) ** block_scale(key_of[2], (ROWS,), ((0, 8),), -0.2, 0.2)), 0.01, 0.1),
        "cross_weight": scatter_about(key_of[3], (E, E), E ** -0.5, 0.375, (), jnp.float32),
        "cross_bias": scatter_about(key_of[4], (E,), 1.0, 4.0, (), jnp.float32),
        "upstream": scatter_about(key_of[5], (SAMPLES, E), 1.0, 6.0, ((0, 32),), jnp.float32),
    }


def reference(bag_ids, table, accum, cross_weight, cross_bias, upstream):
    pooled = lax.optimization_barrier(jnp.sum(jnp.take(table, bag_ids, axis=0), axis=1))
    mixed = jnp.dot(pooled, cross_weight, precision=lax.Precision.HIGHEST) + cross_bias
    crossed = pooled * mixed + pooled
    back = upstream * mixed + jnp.dot(upstream * pooled, cross_weight.T, precision=lax.Precision.HIGHEST) + upstream
    grads = jnp.zeros(table.shape, table.dtype)
    for column in range(BAG):
        grads = grads + jax.ops.segment_sum(back, bag_ids[:, column], num_segments=ROWS)
    new_accum = accum + lax.optimization_barrier(jnp.mean(grads * grads, axis=1))
    new_table = table - 0.5 * grads / jnp.sqrt(new_accum)[:, None]
    return (crossed, new_table, new_accum)
```

```python
import jax
import jax.numpy as jnp
from jax import lax
from jax.experimental import pallas as pl
from jax.experimental.pallas import tpu as pltpu
from jax.sharding import PartitionSpec as P

F32 = jnp.float32
BF16 = jnp.bfloat16
MESH = pl.DeviceIdType.MESH
PLANE = 4
LINE = 4
CHUNK = 256


def split(x):
    hi = x.astype(BF16)
    return hi, (x - hi.astype(F32)).astype(BF16)


def dot(a, b, dims=((1,), (0,))):
    return lax.dot_general(a, b, (dims, ((), ())), preferred_element_type=F32)


def dot3(a, b, dims):
    ah, al = split(a)
    bh, bl = split(b)
    return dot(ah, bh, dims) + (dot(ah, bl, dims) + dot(al, bh, dims))


def kernel(
    bag, ids_ref, table_hbm, accum_ref, weight_ref, bias_ref, up_ref,
    crossed_ref, newt_ref, newa_ref,
    tab, thi, tlo, ids, ct, psend, precv, back, g, grecv,
    load_sem, tab_sem, idz_sem, idp_sem, p_sem, bz_sem, bp_sem, bd_sem, g_sem,
):
    rep = lax.axis_index("rep")
    shard = lax.axis_index("shard")
    z = shard // 2
    core = shard % 2
    rows = tab.shape[1]
    each = up_ref.shape[0]
    mate = (rep, shard + 1 - 2 * core)
    xn = (rep + 1 - 2 * (rep % 2), shard)
    yn = ((rep + 2) % 4, shard)

    def along(k):
        return (rep, ((z + k) % LINE) * 2 + core)

    def send(src, dst, sems, to):
        cp = pltpu.make_async_remote_copy(
            src_ref=src, dst_ref=dst, send_sem=sems.at[0], recv_sem=sems.at[1],
            device_id=to, device_id_type=MESH,
        )
        cp.start()
        return cp

    load = pltpu.make_async_copy(table_hbm, tab.at[0], load_sem)
    load.start()
    ids[0, 0] = ids_ref[...]

    barrier = pltpu.get_barrier_semaphore()
    for to in (mate, xn, yn, along(1), along(2), along(3)):
        pl.semaphore_signal(barrier, inc=1, device_id=to, device_id_type=MESH)
    pl.semaphore_wait(barrier, 6)

    sent = []
    idz = [send(ids_ref, ids.at[0, j], idz_sem.at[j - 1], along(j)) for j in (1, 2, 3)]
    tcp = send(table_hbm, tab.at[1], tab_sem, mate)
    load.wait()
    hi, lo = split(tab[0])
    thi[0:rows] = hi
    tlo[0:rows] = lo
    for cp in idz:
        cp.wait()
    idx = send(ids.at[0], ids.at[1], idp_sem.at[0], xn)
    idy = send(ids.at[0], ids.at[2], idp_sem.at[1], yn)

    own_first = shard * rows
    mate_first = (shard + 1 - 2 * core) * rows
    per_block = rows // CHUNK
    row16 = lax.broadcasted_iota(jnp.int32, (CHUNK, 128), 0).astype(F32).astype(BF16)
    lane = lax.broadcasted_iota(jnp.int32, ids.shape[2:], 1)

    def count(r, p):
        pair = jnp.where(lane < each, ids[r, 2 * p], ids[r, 2 * p + 1])

        def step(q, carry):
            base = jnp.where(q < per_block, own_first, mate_first) + (q % per_block) * CHUNK
            local = pair - base
            local = jnp.where((local >= 0) & (local < CHUNK), local, -1).astype(F32)
            acc = jnp.zeros((CHUNK, 128), BF16)
            for j in range(bag):
                one = jnp.broadcast_to(local[j : j + 1], (16, 128)).astype(BF16)
                wide = jnp.concatenate([one] * (CHUNK // 16), axis=0)
                acc = acc + jnp.where(wide == row16, jnp.ones_like(acc), jnp.zeros_like(acc))
            ct[r, pl.ds(pl.multiple_of(q * CHUNK, CHUNK), CHUNK), pl.ds(p * 128, 128)] = acc
            return carry

        lax.fori_loop(0, 2 * per_block, step, 0)

    count(0, 1)
    count(0, 0)
    tcp.wait()
    hi, lo = split(tab[1])
    thi[rows : 2 * rows] = hi
    tlo[rows : 2 * rows] = lo
    pcp = []
    mine = None
    for p in (1, 0):
        c = ct[0, :, p * 128 : (p + 1) * 128]
        part = dot(c, thi[...], ((0,), (0,))) + dot(c, tlo[...], ((0,), (0,)))
        for h in (0, 1):
            j = 2 * p + h
            block = part[h * each : (h + 1) * each]
            if j == 0:
                mine = block
            else:
                psend[j - 1] = block
                pcp.append(send(psend.at[j - 1], precv.at[j - 1], p_sem.at[j - 1], along(LINE - j)))

    idx.wait()
    idd = send(ids.at[1], ids.at[3], idp_sem.at[2], yn)
    count(1, 0)
    count(1, 1)
    idy.wait()
    count(2, 0)
    count(2, 1)
    idd.wait()
    count(3, 0)
    count(3, 1)

    for cp in pcp:
        cp.wait()
    pooled = (mine + precv[0]) + (precv[1] + precv[2])
    weight = weight_ref[...]
    up = up_ref[...]
    mixed = dot3(pooled, weight, ((1,), (0,))) + bias_ref[...]
    own_back = up * mixed + dot3(up * pooled, weight, ((1,), (1,))) + up
    back[0, 0:each] = own_back

    half = each // 2

    def block(r, j, start=0, size=each):
        return back.at[r, pl.ds(j * each + start, size)]

    zcp = {j: send(block(0, 0), block(0, j), bz_sem.at[j - 1], along(j)) for j in (1, 2, 3)}
    xcp, ycp, dx, dy = {}, {}, {}, {}

    def forward(j):
        xcp[j] = send(block(0, j), block(1, j), bp_sem.at[0, j], xn)
        ycp[j] = send(block(0, j), block(2, j), bp_sem.at[1, j], yn)

    def diagonal(j):
        xcp[j].wait_recv()
        dy[j] = send(block(1, j, 0, half), block(3, j, 0, half), bd_sem.at[0, j], yn)
        ycp[j].wait_recv()
        dx[j] = send(block(2, j, half, half), block(3, j, half, half), bd_sem.at[1, j], xn)

    def product(r):
        bh, bl = split(back[r])
        g[r] = dot(ct[r], bh) + dot(ct[r], bl)

    forward(0)
    crossed_ref[...] = pooled * mixed + pooled
    for j in (1, 2, 3):
        zcp[j].wait_recv()
        forward(j)
        diagonal(j - 1)
    diagonal(3)
    product(0)
    product(1)
    product(2)
    for j in range(LINE):
        dy[j].wait_recv()
        dx[j].wait_recv()
    product(3)
    g[0] = (g[0] + g[1]) + (g[2] + g[3])
    gcp = send(g.at[0, pl.ds(rows, rows)], grecv, g_sem, mate)
    for d in (zcp, xcp, ycp, dx, dy):
        for cp in d.values():
            cp.wait_send()
    gcp.wait()
    total = g[0, 0:rows] + grecv[...]
    mean = jnp.sum(total * total, axis=1, keepdims=True) * (1.0 / total.shape[1])
    acc_col = jnp.transpose(jnp.broadcast_to(accum_ref[...], (8, rows)))[:, 0:1]
    fresh = acc_col + mean
    newt_ref[...] = tab[0] - 0.5 * total * lax.rsqrt(fresh)
    newa_ref[...] = jnp.transpose(jnp.broadcast_to(fresh, (rows, 128)))[0:1]


def fused_body(bag_ids, table, accum, cross_weight, cross_bias, upstream):
    each, bag = bag_ids.shape
    rows, width = table.shape
    tall = -(-bag // 8) * 8
    ids = jnp.pad(bag_ids.T, ((0, tall - bag), (0, 0)), constant_values=-1)
    ids = jnp.concatenate([ids, ids], axis=1)
    vmem = pl.BlockSpec(memory_space=pltpu.VMEM)
    dma = pltpu.SemaphoreType.DMA
    crossed, new_table, new_accum = pl.pallas_call(
        lambda *refs: kernel(bag, *refs),
        out_shape=(
            jax.ShapeDtypeStruct((each, width), F32),
            jax.ShapeDtypeStruct((rows, width), F32),
            jax.ShapeDtypeStruct((1, rows), F32),
        ),
        in_specs=[vmem, pl.BlockSpec(memory_space=pl.ANY), vmem, vmem, vmem, vmem],
        out_specs=(vmem, vmem, vmem),
        scratch_shapes=[
            pltpu.VMEM((2, rows, width), F32),
            pltpu.VMEM((2 * rows, width), BF16),
            pltpu.VMEM((2 * rows, width), BF16),
            pltpu.VMEM((PLANE, LINE, tall, 128), jnp.int32),
            pltpu.VMEM((PLANE, 2 * rows, LINE * each), BF16),
            pltpu.VMEM((LINE - 1, each, width), F32),
            pltpu.VMEM((LINE - 1, each, width), F32),
            pltpu.VMEM((PLANE, LINE * each, width), F32),
            pltpu.VMEM((PLANE, 2 * rows, width), F32),
            pltpu.VMEM((rows, width), F32),
            dma,
            dma((2,)),
            dma((3, 2)),
            dma((3, 2)),
            dma((3, 2)),
            dma((3, 2)),
            dma((2, LINE, 2)),
            dma((2, LINE, 2)),
            dma((2,)),
        ],
        compiler_params=pltpu.CompilerParams(
            collective_id=0, has_side_effects=True, vmem_limit_bytes=40 * 1024 * 1024
        ),
    )(ids, table, accum.reshape(1, rows), cross_weight, cross_bias.reshape(1, width), upstream)
    return crossed, new_table, new_accum.reshape(rows)


def adagrad_rows(rows, sums, grads):
    fresh = sums + jnp.mean(grads * grads, axis=1)
    return (rows - 0.5 * grads / jnp.sqrt(fresh)[:, None], fresh)


def general_body(bag_ids, table, accum, cross_weight, cross_bias, upstream):
    rows_owned = table.shape[0]
    first_row = lax.axis_index("shard") * rows_owned
    group_ids = lax.all_gather(bag_ids, "shard", axis=0, tiled=True)
    local = group_ids - first_row
    number = lax.broadcasted_iota(jnp.int32, (1, rows_owned), 1)
    counts = jnp.zeros((local.shape[0], rows_owned), F32)
    for j in range(local.shape[1]):
        counts = counts + (local[:, j : j + 1] == number).astype(F32)
    pooled = lax.psum_scatter(
        jnp.dot(counts, table, precision=lax.Precision.HIGHEST),
        "shard",
        scatter_dimension=0,
        tiled=True,
    )
    mixed = jnp.dot(pooled, cross_weight, precision=lax.Precision.HIGHEST) + cross_bias
    crossed = pooled * mixed + pooled
    back = (
        upstream * mixed
        + jnp.dot(upstream * pooled, cross_weight.T, precision=lax.Precision.HIGHEST)
        + upstream
    )
    piece = lax.all_gather(back, "shard", axis=0, tiled=True)
    added = lax.dot_general(
        counts, piece, (((0,), (0,)), ((), ())), precision=lax.Precision.HIGHEST
    )
    totals = lax.psum(added, "rep")
    new_table, new_accum = adagrad_rows(table, accum, totals)
    return (crossed, new_table, new_accum)


def solution(mesh):
    placed = (
        P(("rep", "shard"), None),
        P("shard", None),
        P("shard"),
        P(),
        P(),
        P(("rep", "shard"), None),
    )
    small = mesh.shape["rep"] == PLANE and mesh.shape["shard"] == 2 * LINE
    return jax.shard_map(
        fused_body if small else general_body,
        mesh=mesh,
        in_specs=placed,
        out_specs=(P(("rep", "shard"), None), P("shard", None), P("shard")),
        check_vma=False,
    )
```

```python
import jax
import jax.numpy as jnp
from jax import lax
from jax.experimental import pallas as pl
from jax.experimental.pallas import tpu as pltpu
from jax.sharding import PartitionSpec as P

F32 = jnp.float32
BF16 = jnp.bfloat16
MESH = pl.DeviceIdType.MESH
PLANE = 4
LINE = 4
GRANT = 63 * 1024 * 1024
CHUNK = 256


def split(x):
    hi = x.astype(BF16)
    return hi, (x - hi.astype(F32)).astype(BF16)


def dot(a, b, dims=((1,), (0,))):
    return lax.dot_general(a, b, (dims, ((), ())), preferred_element_type=F32)


def kernel(
    bag, ids_hbm, table_hbm, accum_hbm, weight_hbm, bias_hbm, up_hbm,
    crossed_out, newt_out, newa_out,
    tab, thi, tlo, ids, ct, psend, precv, back, g, grecv,
    ids_raw, accum, weight, bias, up, wsp, crossed_ref, newt_ref, newa_ref,
    load_sem, store_sem, tab_sem, idz_sem, idp_sem, p_sem, bz_sem, bp_sem, bd_sem, g_sem,
):
    rep = lax.axis_index("rep")
    shard = lax.axis_index("shard")
    z = shard // 2
    core = shard % 2
    rows = tab.shape[1]
    each = up.shape[0]
    mate = (rep, shard + 1 - 2 * core)
    xn = (rep + 1 - 2 * (rep % 2), shard)
    yn = ((rep + 2) % 4, shard)
    line = {
        1: (rep, (z + 1 - 2 * (z % 2)) * 2 + core),
        2: (rep, ((z + 2) % LINE) * 2 + core),
        3: (rep, (LINE - 1 - z) * 2 + core),
    }

    def send(src, dst, sems, to):
        cp = pltpu.make_async_remote_copy(
            src_ref=src, dst_ref=dst, send_sem=sems.at[0], recv_sem=sems.at[1],
            device_id=to, device_id_type=MESH,
        )
        cp.start()
        return cp

    barrier = pltpu.get_barrier_semaphore()
    for to in (mate, xn, yn, line[1], line[2], line[3]):
        pl.semaphore_signal(barrier, inc=1, device_id=to, device_id_type=MESH)

    def load(src, dst, i):
        cp = pltpu.make_async_copy(src, dst, load_sem.at[i])
        cp.start()
        return cp

    ids_load = load(ids_hbm, ids_raw, 0)
    table_load = load(table_hbm, tab.at[0], 1)
    rest = [
        load(src, dst, 2 + i)
        for i, (src, dst) in enumerate(
            ((weight_hbm, weight), (up_hbm, up), (bias_hbm, bias), (accum_hbm, accum))
        )
    ]
    ids_load.wait()
    raw = ids_raw[...]
    ids[0, 0] = jnp.full(ids.shape[2:], -1, jnp.int32)
    ids[0, 0, 0:bag] = jnp.concatenate([raw, raw], axis=1)
    pl.semaphore_wait(barrier, 6)

    idz = {j: send(ids.at[0, 0], ids.at[0, j], idz_sem.at[j - 1], line[j]) for j in (2, 3, 1)}
    tcp = send(table_hbm, tab.at[1], tab_sem, mate)
    table_load.wait()
    hi, lo = split(tab[0])
    thi[0:rows] = hi
    tlo[0:rows] = lo

    own_first = shard * rows
    mate_first = (shard + 1 - 2 * core) * rows
    per_block = rows // CHUNK
    row16 = lax.broadcasted_iota(jnp.int32, (CHUNK, 128), 0).astype(F32).astype(BF16)
    lane = lax.broadcasted_iota(jnp.int32, ids.shape[2:], 1)

    def count(r, p):
        pair = jnp.where(lane < each, ids[r, 2 * p], ids[r, 2 * p + 1])

        def step(q, carry):
            base = jnp.where(q < per_block, own_first, mate_first) + (q % per_block) * CHUNK
            local = pair - base
            local = jnp.where((local >= 0) & (local < CHUNK), local, -1).astype(F32)
            acc = jnp.zeros((CHUNK, 128), BF16)
            for j in range(bag):
                one = jnp.broadcast_to(local[j : j + 1], (16, 128)).astype(BF16)
                wide = jnp.concatenate([one] * (CHUNK // 16), axis=0)
                acc = acc + jnp.where(wide == row16, jnp.ones_like(acc), jnp.zeros_like(acc))
            ct[r, pl.ds(pl.multiple_of(q * CHUNK, CHUNK), CHUNK), pl.ds(p * 128, 128)] = acc
            return carry

        lax.fori_loop(0, 2 * per_block, step, 0)

    pcp = {}
    mine = None
    for p in (1, 0):
        for j in ((2, 3) if p else (1,)):
            idz[j].wait()
        if not p:
            idx = send(ids.at[0], ids.at[1], idp_sem.at[0], xn)
            idy = send(ids.at[0], ids.at[2], idp_sem.at[1], yn)
        count(0, p)
        if p:
            tcp.wait()
            hi, lo = split(tab[1])
            thi[rows : 2 * rows] = hi
            tlo[rows : 2 * rows] = lo
        c = ct[0, :, p * 128 : (p + 1) * 128]
        part = dot(c, thi[...], ((0,), (0,))) + dot(c, tlo[...], ((0,), (0,)))
        for h in (0, 1):
            j = 2 * p + h
            block = part[h * each : (h + 1) * each]
            if j == 0:
                mine = block
            else:
                psend[j - 1] = block
                pcp[j] = send(psend.at[j - 1], precv.at[j - 1], p_sem.at[j - 1], line[j])

    idx.wait()
    idd = send(ids.at[1], ids.at[3], idp_sem.at[2], yn)
    for cp in rest:
        cp.wait()
    hi, lo = split(weight[...])
    wsp[0] = hi
    wsp[1] = lo
    turned = jnp.transpose(weight[...])
    hi, lo = split(turned)
    wsp[2] = hi
    wsp[3] = lo
    count(1, 0)
    count(1, 1)
    idy.wait()
    count(2, 0)
    count(2, 1)
    idd.wait()
    count(3, 0)
    count(3, 1)

    for cp in pcp.values():
        cp.wait()
    pooled = (mine + precv[0]) + (precv[1] + precv[2])

    def cross(x, k):
        xh, xl = split(x)
        return dot(xh, wsp[k]) + (dot(xh, wsp[k + 1]) + dot(xl, wsp[k]))

    grad = up[...]
    mixed = cross(pooled, 0) + bias[...]
    back[0, 0:each] = grad * mixed + cross(grad * pooled, 2) + grad

    half = each // 2

    def block(r, j, start=0, size=each):
        return back.at[r, pl.ds(j * each + start, size)]

    xcp, ycp, dx, dy = {}, {}, {}, {}

    def forward(j):
        xcp[j] = send(block(0, j), block(1, j), bp_sem.at[0, j], xn)
        ycp[j] = send(block(0, j), block(2, j), bp_sem.at[1, j], yn)

    def diagonal(j):
        xcp[j].wait_recv()
        dy[j] = send(block(1, j, 0, half), block(3, j, 0, half), bd_sem.at[0, j], yn)
        ycp[j].wait_recv()
        dx[j] = send(block(2, j, half, half), block(3, j, half, half), bd_sem.at[1, j], xn)

    zcp = {j: send(block(0, 0), block(0, j), bz_sem.at[j - 1], line[j]) for j in (2, 1)}
    forward(0)
    crossed_ref[...] = pooled * mixed + pooled
    stores = [pltpu.make_async_copy(crossed_ref, crossed_out, store_sem.at[0])]
    stores[0].start()
    zcp[1].wait_recv()
    forward(1)
    diagonal(0)
    zcp[2].wait_recv()
    zcp[3] = send(block(0, 2), block(0, 3), bz_sem.at[2], line[1])
    forward(2)
    diagonal(1)
    zcp[3].wait_recv()
    forward(3)
    diagonal(2)
    diagonal(3)

    def product(r, start=0, size=2 * rows):
        bh, bl = split(back[r])
        c = ct[r, start : start + size]
        g[r, start : start + size] = dot(c, bh) + dot(c, bl)

    product(0)
    product(1)
    product(2)
    for j in range(LINE):
        dy[j].wait_recv()
        dx[j].wait_recv()

    def finish(start, size):
        product(3, start, size)
        at = slice(start, start + size)
        g[0, at] = (g[0, at] + g[1, at]) + (g[2, at] + g[3, at])

    piece = rows // 2
    gcp = []
    for i in range(2):
        finish(rows + i * piece, piece)
        gcp.append(
            send(g.at[0, pl.ds(rows + i * piece, piece)], grecv.at[pl.ds(i * piece, piece)], g_sem.at[i], mate)
        )
    finish(0, rows)
    acc_col = jnp.transpose(jnp.broadcast_to(accum[...], (8, rows)))[:, 0:1]
    for d in (zcp, xcp, ycp, dx, dy):
        for cp in d.values():
            cp.wait_send()
    for i in range(2):
        gcp[i].wait()
        at = slice(i * piece, (i + 1) * piece)
        total = g[0, at] + grecv[at]
        mean = jnp.sum(total * total, axis=1, keepdims=True) * (1.0 / total.shape[1])
        fresh = acc_col[at] + mean
        newt_ref[at] = tab[0, at] - 0.5 * total * lax.rsqrt(fresh)
        part = pl.ds(i * piece, piece)
        stores.append(pltpu.make_async_copy(newt_ref.at[part], newt_out.at[part], store_sem.at[1 + i]))
        stores[-1].start()
        newa_ref[:, at] = jnp.transpose(jnp.broadcast_to(fresh, (piece, 128)))[0:1]
    stores.append(pltpu.make_async_copy(newa_ref, newa_out, store_sem.at[3]))
    stores[-1].start()
    for cp in stores:
        cp.wait()


def hand_out(a, b, c, x, y, w, sems):
    copies = [
        pltpu.make_async_copy(src, dst, sems.at[i])
        for i, (src, dst) in enumerate(((b, y), (a, x), (c, w)))
    ]
    for cp in copies:
        cp.start()
    for cp in copies:
        cp.wait()


def fused_body(bag_ids, table, accum, cross_weight, cross_bias, upstream):
    each, bag = bag_ids.shape
    rows, width = table.shape
    tall = -(-bag // 8) * 8
    hbm = pl.BlockSpec(memory_space=pltpu.HBM)
    dma = pltpu.SemaphoreType.DMA
    shapes = (
        jax.ShapeDtypeStruct((each, width), F32),
        jax.ShapeDtypeStruct((rows, width), F32),
        jax.ShapeDtypeStruct((1, rows), F32),
    )
    done = pl.pallas_call(
        lambda *refs: kernel(bag, *refs),
        out_shape=shapes,
        in_specs=[hbm] * 6,
        out_specs=[hbm] * 3,
        scratch_shapes=[
            pltpu.VMEM((2, rows, width), F32),
            pltpu.VMEM((2 * rows, width), BF16),
            pltpu.VMEM((2 * rows, width), BF16),
            pltpu.VMEM((PLANE, LINE, tall, 128), jnp.int32),
            pltpu.VMEM((PLANE, 2 * rows, LINE * each), BF16),
            pltpu.VMEM((LINE - 1, each, width), F32),
            pltpu.VMEM((LINE - 1, each, width), F32),
            pltpu.VMEM((PLANE, LINE * each, width), F32),
            pltpu.VMEM((PLANE, 2 * rows, width), F32),
            pltpu.VMEM((rows, width), F32),
            pltpu.VMEM((bag, each), jnp.int32),
            pltpu.VMEM((1, rows), F32),
            pltpu.VMEM((width, width), F32),
            pltpu.VMEM((1, width), F32),
            pltpu.VMEM((each, width), F32),
            pltpu.VMEM((4, width, width), BF16),
            pltpu.VMEM((each, width), F32),
            pltpu.VMEM((rows, width), F32),
            pltpu.VMEM((1, rows), F32),
            dma((6,)),
            dma((4,)),
            dma((2,)),
            dma((3, 2)),
            dma((3, 2)),
            dma((3, 2)),
            dma((3, 2)),
            dma((2, LINE, 2)),
            dma((2, LINE, 2)),
            dma((2, 2)),
        ],
        compiler_params=pltpu.CompilerParams(
            collective_id=0, has_side_effects=True, vmem_limit_bytes=GRANT
        ),
    )(bag_ids.T, table, accum.reshape(1, rows), cross_weight, cross_bias.reshape(1, width), upstream)
    crossed, new_table, new_accum = pl.pallas_call(
        hand_out,
        out_shape=shapes,
        in_specs=[hbm] * 3,
        out_specs=[hbm] * 3,
        scratch_shapes=[dma((3,))],
        compiler_params=pltpu.CompilerParams(vmem_limit_bytes=GRANT),
    )(*done)
    return crossed, new_table, new_accum.reshape(rows)


def adagrad_rows(rows, sums, grads):
    fresh = sums + jnp.mean(grads * grads, axis=1)
    return (rows - 0.5 * grads / jnp.sqrt(fresh)[:, None], fresh)


def general_body(bag_ids, table, accum, cross_weight, cross_bias, upstream):
    rows_owned = table.shape[0]
    first_row = lax.axis_index("shard") * rows_owned
    group_ids = lax.all_gather(bag_ids, "shard", axis=0, tiled=True)
    local = group_ids - first_row
    number = lax.broadcasted_iota(jnp.int32, (1, rows_owned), 1)
    counts = jnp.zeros((local.shape[0], rows_owned), F32)
    for j in range(local.shape[1]):
        counts = counts + (local[:, j : j + 1] == number).astype(F32)
    pooled = lax.psum_scatter(
        jnp.dot(counts, table, precision=lax.Precision.HIGHEST),
        "shard",
        scatter_dimension=0,
        tiled=True,
    )
    mixed = jnp.dot(pooled, cross_weight, precision=lax.Precision.HIGHEST) + cross_bias
    crossed = pooled * mixed + pooled
    back = (
        upstream * mixed
        + jnp.dot(upstream * pooled, cross_weight.T, precision=lax.Precision.HIGHEST)
        + upstream
    )
    piece = lax.all_gather(back, "shard", axis=0, tiled=True)
    added = lax.dot_general(
        counts, piece, (((0,), (0,)), ((), ())), precision=lax.Precision.HIGHEST
    )
    totals = lax.psum(added, "rep")
    new_table, new_accum = adagrad_rows(table, accum, totals)
    return (crossed, new_table, new_accum)


def solution(mesh):
    placed = (
        P(("rep", "shard"), None),
        P("shard", None),
        P("shard"),
        P(),
        P(),
        P(("rep", "shard"), None),
    )
    small = mesh.shape["rep"] == PLANE and mesh.shape["shard"] == 2 * LINE
    return jax.shard_map(
        fused_body if small else general_body,
        mesh=mesh,
        in_specs=placed,
        out_specs=(P(("rep", "shard"), None), P("shard", None), P("shard")),
        check_vma=False,
    )
```

```python
import jax
import jax.numpy as jnp
from jax import lax
from jax.experimental import pallas as pl
from jax.experimental.pallas import tpu as pltpu
from jax.sharding import PartitionSpec as P

F32 = jnp.float32
BF16 = jnp.bfloat16
MESH = pl.DeviceIdType.MESH
PLANE = 4
LINE = 4
GRANT = 63 * 1024 * 1024
CHUNK = 256


def split(x):
    hi = x.astype(BF16)
    return hi, (x - hi.astype(F32)).astype(BF16)


def dot(a, b, dims=((1,), (0,))):
    return lax.dot_general(a, b, (dims, ((), ())), preferred_element_type=F32)


def kernel(
    bag, ids_hbm, table_hbm, accum_hbm, weight_hbm, bias_hbm, up_hbm,
    crossed_out, newt_out, newa_out,
    tab, thi, tlo, ids, ct, psend, precv, back, g, grecv,
    ids_raw, accum, weight, bias, up, wsp, crossed_ref, newt_ref, newa_ref,
    load_sem, store_sem, tab_sem, idz_sem, idp_sem, p_sem, bz_sem, bp_sem, bd_sem, g_sem,
):
    rep = lax.axis_index("rep")
    shard = lax.axis_index("shard")
    z = shard // 2
    core = shard % 2
    rows = tab.shape[1]
    each = up.shape[0]
    mate = (rep, shard + 1 - 2 * core)
    xn = (rep + 1 - 2 * (rep % 2), shard)
    yn = ((rep + 2) % 4, shard)
    line = {
        1: (rep, (z + 1 - 2 * (z % 2)) * 2 + core),
        2: (rep, ((z + 2) % LINE) * 2 + core),
        3: (rep, (LINE - 1 - z) * 2 + core),
    }

    def send(src, dst, sems, to):
        cp = pltpu.make_async_remote_copy(
            src_ref=src, dst_ref=dst, send_sem=sems.at[0], recv_sem=sems.at[1],
            device_id=to, device_id_type=MESH,
        )
        cp.start()
        return cp

    barrier = pltpu.get_barrier_semaphore()
    for to in (mate, xn, yn, line[1], line[2], line[3]):
        pl.semaphore_signal(barrier, inc=1, device_id=to, device_id_type=MESH)

    def load(src, dst, i):
        cp = pltpu.make_async_copy(src, dst, load_sem.at[i])
        cp.start()
        return cp

    ids_load = load(ids_hbm, ids_raw, 0)
    table_load = load(table_hbm, tab.at[0], 1)
    rest = [
        load(src, dst, 2 + i)
        for i, (src, dst) in enumerate(
            ((weight_hbm, weight), (up_hbm, up), (bias_hbm, bias), (accum_hbm, accum))
        )
    ]
    ids_load.wait()
    raw = ids_raw[...]
    ids[0, 0] = jnp.full(ids.shape[2:], -1, jnp.int32)
    ids[0, 0, 0:bag] = jnp.concatenate([raw, raw], axis=1)
    pl.semaphore_wait(barrier, 6)

    idz = {j: send(ids.at[0, 0], ids.at[0, j], idz_sem.at[j - 1], line[j]) for j in (2, 3, 1)}
    tcp = send(table_hbm, tab.at[1], tab_sem, mate)
    table_load.wait()
    hi, lo = split(tab[0])
    thi[0:rows] = hi
    tlo[0:rows] = lo

    own_first = shard * rows
    mate_first = (shard + 1 - 2 * core) * rows
    per_block = rows // CHUNK
    row16 = lax.broadcasted_iota(jnp.int32, (CHUNK, 128), 0).astype(F32).astype(BF16)
    lane = lax.broadcasted_iota(jnp.int32, ids.shape[2:], 1)

    def count(r, p):
        pair = jnp.where(lane < each, ids[r, 2 * p], ids[r, 2 * p + 1])

        def step(q, carry):
            base = jnp.where(q < per_block, own_first, mate_first) + (q % per_block) * CHUNK
            local = pair - base
            local = jnp.where((local >= 0) & (local < CHUNK), local, -1).astype(F32)
            acc = jnp.zeros((CHUNK, 128), BF16)
            for j in range(bag):
                one = jnp.broadcast_to(local[j : j + 1], (16, 128)).astype(BF16)
                wide = jnp.concatenate([one] * (CHUNK // 16), axis=0)
                away = wide - row16
                acc = acc + jnp.minimum(away * away, jnp.ones_like(acc))
            met = jnp.full_like(acc, bag) - acc
            ct[r, pl.ds(pl.multiple_of(q * CHUNK, CHUNK), CHUNK), pl.ds(p * 128, 128)] = met
            return carry

        lax.fori_loop(0, 2 * per_block, step, 0)

    pcp = {}
    mine = None
    for p in (1, 0):
        for j in ((2, 3) if p else (1,)):
            idz[j].wait()
        if not p:
            idx = send(ids.at[0], ids.at[1], idp_sem.at[0], xn)
            idy = send(ids.at[0], ids.at[2], idp_sem.at[1], yn)
        count(0, p)
        if p:
            tcp.wait()
            hi, lo = split(tab[1])
            thi[rows : 2 * rows] = hi
            tlo[rows : 2 * rows] = lo
        c = ct[0, :, p * 128 : (p + 1) * 128]
        part = dot(c, thi[...], ((0,), (0,))) + dot(c, tlo[...], ((0,), (0,)))
        for h in (0, 1):
            j = 2 * p + h
            block = part[h * each : (h + 1) * each]
            if j == 0:
                mine = block
            else:
                psend[j - 1] = block
                pcp[j] = send(psend.at[j - 1], precv.at[j - 1], p_sem.at[j - 1], line[j])

    idx.wait()
    idd = send(ids.at[1], ids.at[3], idp_sem.at[2], yn)
    for cp in rest:
        cp.wait()
    hi, lo = split(weight[...])
    wsp[0] = hi
    wsp[1] = lo
    turned = jnp.transpose(weight[...])
    hi, lo = split(turned)
    wsp[2] = hi
    wsp[3] = lo
    count(1, 0)
    count(1, 1)
    idy.wait()
    count(2, 0)
    count(2, 1)
    idd.wait()
    count(3, 0)
    count(3, 1)

    for cp in pcp.values():
        cp.wait()
    pooled = (mine + precv[0]) + (precv[1] + precv[2])

    def cross(x, k):
        xh, xl = split(x)
        return dot(xh, wsp[k]) + (dot(xh, wsp[k + 1]) + dot(xl, wsp[k]))

    grad = up[...]
    mixed = cross(pooled, 0) + bias[...]
    back[0, 0:each] = grad * mixed + cross(grad * pooled, 2) + grad

    half = each // 2

    def block(r, j, start=0, size=each):
        return back.at[r, pl.ds(j * each + start, size)]

    xcp, ycp, dx, dy = {}, {}, {}, {}

    def forward(j):
        xcp[j] = send(block(0, j), block(1, j), bp_sem.at[0, j], xn)
        ycp[j] = send(block(0, j), block(2, j), bp_sem.at[1, j], yn)

    def diagonal(j):
        xcp[j].wait_recv()
        dy[j] = send(block(1, j, 0, half), block(3, j, 0, half), bd_sem.at[0, j], yn)
        ycp[j].wait_recv()
        dx[j] = send(block(2, j, half, half), block(3, j, half, half), bd_sem.at[1, j], xn)

    zcp = {j: send(block(0, 0), block(0, j), bz_sem.at[j - 1], line[j]) for j in (2, 1)}
    forward(0)
    crossed_ref[...] = pooled * mixed + pooled
    stores = [pltpu.make_async_copy(crossed_ref, crossed_out, store_sem.at[0])]
    stores[0].start()
    zcp[1].wait_recv()
    forward(1)
    diagonal(0)
    zcp[2].wait_recv()
    zcp[3] = send(block(0, 2), block(0, 3), bz_sem.at[2], line[1])
    forward(2)
    diagonal(1)
    zcp[3].wait_recv()
    forward(3)
    diagonal(2)
    diagonal(3)

    def product(r, start=0, size=2 * rows):
        bh, bl = split(back[r])
        c = ct[r, start : start + size]
        g[r, start : start + size] = dot(c, bh) + dot(c, bl)

    product(0)
    product(1)
    product(2)
    for j in range(LINE):
        dy[j].wait_recv()
        dx[j].wait_recv()

    def finish(start, size):
        product(3, start, size)
        at = slice(start, start + size)
        g[0, at] = (g[0, at] + g[1, at]) + (g[2, at] + g[3, at])

    piece = rows // 2
    gcp = []
    for i in range(2):
        finish(rows + i * piece, piece)
        gcp.append(
            send(g.at[0, pl.ds(rows + i * piece, piece)], grecv.at[pl.ds(i * piece, piece)], g_sem.at[i], mate)
        )
    finish(0, rows)
    acc_col = jnp.transpose(jnp.broadcast_to(accum[...], (8, rows)))[:, 0:1]
    for d in (zcp, xcp, ycp, dx, dy):
        for cp in d.values():
            cp.wait_send()
    for i in range(2):
        gcp[i].wait()
        at = slice(i * piece, (i + 1) * piece)
        total = g[0, at] + grecv[at]
        mean = jnp.sum(total * total, axis=1, keepdims=True) * (1.0 / total.shape[1])
        fresh = acc_col[at] + mean
        newt_ref[at] = tab[0, at] - 0.5 * total * lax.rsqrt(fresh)
        part = pl.ds(i * piece, piece)
        stores.append(pltpu.make_async_copy(newt_ref.at[part], newt_out.at[part], store_sem.at[1 + i]))
        stores[-1].start()
        newa_ref[:, at] = jnp.transpose(jnp.broadcast_to(fresh, (piece, 128)))[0:1]
    stores.append(pltpu.make_async_copy(newa_ref, newa_out, store_sem.at[3]))
    stores[-1].start()
    for cp in stores:
        cp.wait()


def hand_out(a, b, c, x, y, w, va, vb, vc, sems_in, sems_out):
    piece = vb.shape[0] // 2
    parts = [(b.at[pl.ds(i * piece, piece)], vb.at[pl.ds(i * piece, piece)], y.at[pl.ds(i * piece, piece)]) for i in (0, 1)]
    parts += [(a, va, x), (c, vc, w)]
    ins = [pltpu.make_async_copy(p[0], p[1], sems_in.at[i]) for i, p in enumerate(parts)]
    outs = [pltpu.make_async_copy(p[1], p[2], sems_out.at[i]) for i, p in enumerate(parts)]
    for cp in ins:
        cp.start()
    for cp, out in zip(ins, outs):
        cp.wait()
        out.start()
    for cp in outs:
        cp.wait()


def fused_body(bag_ids, table, accum, cross_weight, cross_bias, upstream):
    each, bag = bag_ids.shape
    rows, width = table.shape
    tall = -(-bag // 8) * 8
    hbm = pl.BlockSpec(memory_space=pltpu.HBM)
    dma = pltpu.SemaphoreType.DMA
    shapes = (
        jax.ShapeDtypeStruct((each, width), F32),
        jax.ShapeDtypeStruct((rows, width), F32),
        jax.ShapeDtypeStruct((1, rows), F32),
    )
    done = pl.pallas_call(
        lambda *refs: kernel(bag, *refs),
        out_shape=shapes,
        in_specs=[hbm] * 6,
        out_specs=[hbm] * 3,
        scratch_shapes=[
            pltpu.VMEM((2, rows, width), F32),
            pltpu.VMEM((2 * rows, width), BF16),
            pltpu.VMEM((2 * rows, width), BF16),
            pltpu.VMEM((PLANE, LINE, tall, 128), jnp.int32),
            pltpu.VMEM((PLANE, 2 * rows, LINE * each), BF16),
            pltpu.VMEM((LINE - 1, each, width), F32),
            pltpu.VMEM((LINE - 1, each, width), F32),
            pltpu.VMEM((PLANE, LINE * each, width), F32),
            pltpu.VMEM((PLANE, 2 * rows, width), F32),
            pltpu.VMEM((rows, width), F32),
            pltpu.VMEM((bag, each), jnp.int32),
            pltpu.VMEM((1, rows), F32),
            pltpu.VMEM((width, width), F32),
            pltpu.VMEM((1, width), F32),
            pltpu.VMEM((each, width), F32),
            pltpu.VMEM((4, width, width), BF16),
            pltpu.VMEM((each, width), F32),
            pltpu.VMEM((rows, width), F32),
            pltpu.VMEM((1, rows), F32),
            dma((6,)),
            dma((4,)),
            dma((2,)),
            dma((3, 2)),
            dma((3, 2)),
            dma((3, 2)),
            dma((3, 2)),
            dma((2, LINE, 2)),
            dma((2, LINE, 2)),
            dma((2, 2)),
        ],
        compiler_params=pltpu.CompilerParams(
            collective_id=0, has_side_effects=True, vmem_limit_bytes=GRANT
        ),
    )(bag_ids.T, table, accum.reshape(1, rows), cross_weight, cross_bias.reshape(1, width), upstream)
    crossed, new_table, new_accum = pl.pallas_call(
        hand_out,
        out_shape=shapes,
        in_specs=[hbm] * 3,
        out_specs=[hbm] * 3,
        scratch_shapes=[pltpu.VMEM(a.shape, F32) for a in shapes] + [dma((4,)), dma((4,))],
        compiler_params=pltpu.CompilerParams(vmem_limit_bytes=GRANT),
    )(*done)
    return crossed, new_table, new_accum.reshape(rows)


def adagrad_rows(rows, sums, grads):
    fresh = sums + jnp.mean(grads * grads, axis=1)
    return (rows - 0.5 * grads / jnp.sqrt(fresh)[:, None], fresh)


def general_body(bag_ids, table, accum, cross_weight, cross_bias, upstream):
    rows_owned = table.shape[0]
    first_row = lax.axis_index("shard") * rows_owned
    group_ids = lax.all_gather(bag_ids, "shard", axis=0, tiled=True)
    local = group_ids - first_row
    number = lax.broadcasted_iota(jnp.int32, (1, rows_owned), 1)
    counts = jnp.zeros((local.shape[0], rows_owned), F32)
    for j in range(local.shape[1]):
        counts = counts + (local[:, j : j + 1] == number).astype(F32)
    pooled = lax.psum_scatter(
        jnp.dot(counts, table, precision=lax.Precision.HIGHEST),
        "shard",
        scatter_dimension=0,
        tiled=True,
    )
    mixed = jnp.dot(pooled, cross_weight, precision=lax.Precision.HIGHEST) + cross_bias
    crossed = pooled * mixed + pooled
    back = (
        upstream * mixed
        + jnp.dot(upstream * pooled, cross_weight.T, precision=lax.Precision.HIGHEST)
        + upstream
    )
    piece = lax.all_gather(back, "shard", axis=0, tiled=True)
    added = lax.dot_general(
        counts, piece, (((0,), (0,)), ((), ())), precision=lax.Precision.HIGHEST
    )
    totals = lax.psum(added, "rep")
    new_table, new_accum = adagrad_rows(table, accum, totals)
    return (crossed, new_table, new_accum)


def solution(mesh):
    placed = (
        P(("rep", "shard"), None),
        P("shard", None),
        P("shard"),
        P(),
        P(),
        P(("rep", "shard"), None),
    )
    small = mesh.shape["rep"] == PLANE and mesh.shape["shard"] == 2 * LINE
    return jax.shard_map(
        fused_body if small else general_body,
        mesh=mesh,
        in_specs=placed,
        out_specs=(P(("rep", "shard"), None), P("shard", None), P("shard")),
        check_vma=False,
    )
```

```python
import jax
import jax.numpy as jnp
from jax import lax
from jax.experimental import pallas as pl
from jax.experimental.pallas import tpu as pltpu
from jax.sharding import PartitionSpec as P

F32 = jnp.float32
BF16 = jnp.bfloat16
MESH = pl.DeviceIdType.MESH
PLANE = 4
LINE = 4
GRANT = 63 * 1024 * 1024
CHUNK = 256


def split(x):
    hi = x.astype(BF16)
    return hi, (x - hi.astype(F32)).astype(BF16)


def dot(a, b, dims=((1,), (0,))):
    return lax.dot_general(a, b, (dims, ((), ())), preferred_element_type=F32)


def kernel(
    bag, ids_hbm, table_hbm, accum_hbm, weight_hbm, bias_hbm, up_hbm,
    crossed_out, newt_out, newa_out,
    tab, thi, tlo, ids, ct, psend, precv, back, g, grecv,
    ids_raw, accum, weight, bias, up, wsp, crossed_ref, newt_ref, newa_ref,
    load_sem, store_sem, tab_sem, idz_sem, idp_sem, p_sem, bz_sem, bp_sem, bd_sem, g_sem,
):
    rep = lax.axis_index("rep")
    shard = lax.axis_index("shard")
    z = shard // 2
    core = shard % 2
    rows = tab.shape[1]
    each = up.shape[0]
    mate = (rep, shard + 1 - 2 * core)
    xn = (rep + 1 - 2 * (rep % 2), shard)
    yn = ((rep + 2) % 4, shard)
    line = {
        1: (rep, (z + 1 - 2 * (z % 2)) * 2 + core),
        2: (rep, ((z + 2) % LINE) * 2 + core),
        3: (rep, (LINE - 1 - z) * 2 + core),
    }

    def send(src, dst, sems, to):
        cp = pltpu.make_async_remote_copy(
            src_ref=src, dst_ref=dst, send_sem=sems.at[0], recv_sem=sems.at[1],
            device_id=to, device_id_type=MESH,
        )
        cp.start()
        return cp

    barrier = pltpu.get_barrier_semaphore()
    for to in (mate, xn, yn, line[1], line[2], line[3]):
        pl.semaphore_signal(barrier, inc=1, device_id=to, device_id_type=MESH)

    def load(src, dst, i):
        cp = pltpu.make_async_copy(src, dst, load_sem.at[i])
        cp.start()
        return cp

    ids_load = load(ids_hbm, ids_raw, 0)
    table_load = load(table_hbm, tab.at[0], 1)
    rest = [
        load(src, dst, 2 + i)
        for i, (src, dst) in enumerate(
            ((weight_hbm, weight), (up_hbm, up), (bias_hbm, bias), (accum_hbm, accum))
        )
    ]
    ids_load.wait()
    raw = ids_raw[...]
    ids[0, 0] = jnp.full(ids.shape[2:], -1, jnp.int32)
    ids[0, 0, 0:bag] = jnp.concatenate([raw, raw], axis=1)
    pl.semaphore_wait(barrier, 6)

    idz = {j: send(ids.at[0, 0], ids.at[0, j], idz_sem.at[j - 1], line[j]) for j in (2, 3, 1)}
    tcp = send(table_hbm, tab.at[1], tab_sem, mate)
    table_load.wait()
    hi, lo = split(tab[0])
    thi[0:rows] = hi
    tlo[0:rows] = lo

    for cp in rest:
        cp.wait()
    hi, lo = split(weight[...])
    wsp[0] = hi
    wsp[1] = lo
    turned = jnp.transpose(weight[...])
    hi, lo = split(turned)
    wsp[2] = hi
    wsp[3] = lo

    own_first = shard * rows
    mate_first = (shard + 1 - 2 * core) * rows
    per_block = rows // CHUNK
    row16 = lax.broadcasted_iota(jnp.int32, (CHUNK, 128), 0).astype(F32).astype(BF16)
    lane = lax.broadcasted_iota(jnp.int32, ids.shape[2:], 1)
    spot = lax.broadcasted_iota(jnp.int32, ids.shape[2:], 0)
    half = each // 2

    def count(r, p):
        pair = jnp.where(lane < each, ids[r, 2 * p], ids[r, 2 * p + 1])
        times = jnp.ones(pair.shape, F32)
        for i in range(bag - 1):
            again = (spot > i) & (pair == pair[i : i + 1])
            times = times + jnp.where(again, 1.0, 0.0)

        def widen(row):
            one = jnp.broadcast_to(row, (16, 128)).astype(BF16)
            return jnp.concatenate([one] * (CHUNK // 16), axis=0)

        def step(q, carry):
            base = jnp.where(q < per_block, own_first, mate_first) + (q % per_block) * CHUNK
            local = pair - base
            local = jnp.where((local >= 0) & (local < CHUNK), local, -1).astype(F32)
            acc = jnp.zeros((CHUNK, 128), BF16)
            for j in range(bag):
                acc = jnp.where(widen(local[j : j + 1]) == row16, widen(times[j : j + 1]), acc)
            ct[r, pl.ds(pl.multiple_of(q * CHUNK, CHUNK), CHUNK), pl.ds(p * 128, 128)] = acc
            return carry

        lax.fori_loop(0, 2 * per_block, step, 0)

    pcp = {}
    mine = None

    def give(j, h):
        part = pl.ds(h * half, half)
        pcp[j, h] = send(psend.at[j - 1, part], precv.at[j - 1, part], p_sem.at[j - 1, h], line[j])

    for p in (1, 0):
        for j in ((2, 3) if p else (1,)):
            idz[j].wait()
        if not p:
            idx = send(ids.at[0], ids.at[1], idp_sem.at[0], xn)
            idy = send(ids.at[0], ids.at[2], idp_sem.at[1], yn)
        count(0, p)
        if p:
            tcp.wait()
            hi, lo = split(tab[1])
            thi[rows : 2 * rows] = hi
            tlo[rows : 2 * rows] = lo
        c = ct[0, :, p * 128 : (p + 1) * 128]
        part = dot(c, thi[...], ((0,), (0,))) + dot(c, tlo[...], ((0,), (0,)))
        for i in (0, 1):
            j = 2 * p + i
            piece = part[i * each : (i + 1) * each]
            if j == 0:
                mine = piece
            else:
                psend[j - 1] = piece
                give(j, 0)
    for j in (2, 3, 1):
        give(j, 1)

    idx.wait()
    idd = send(ids.at[1], ids.at[3], idp_sem.at[2], yn)
    count(1, 0)
    count(1, 1)

    def cross(x, k):
        xh, xl = split(x)
        return dot(xh, wsp[k]) + (dot(xh, wsp[k + 1]) + dot(xl, wsp[k]))

    def block(r, j, h):
        return back.at[r, pl.ds(j * each + h * half, half)]

    zcp, xcp, ycp, dcp = {}, {}, {}, {}

    def forward(j, h):
        xcp[j, h] = send(block(0, j, h), block(1, j, h), bp_sem.at[0, j, h], xn)
        ycp[j, h] = send(block(0, j, h), block(2, j, h), bp_sem.at[1, j, h], yn)

    def process(h):
        at = slice(h * half, (h + 1) * half)
        for j in (1, 2, 3):
            pcp[j, h].wait()
        pooled = (mine[at] + precv[0, at]) + (precv[1, at] + precv[2, at])
        grad = up[at]
        mixed = cross(pooled, 0) + bias[...]
        back[0, at] = grad * mixed + cross(grad * pooled, 2) + grad
        for j in (2, 1):
            zcp[j, h] = send(block(0, 0, h), block(0, j, h), bz_sem.at[j - 1, h], line[j])
        forward(0, h)
        crossed_ref[at] = pooled * mixed + pooled

    def along(j, h):
        zcp[j, h].wait_recv()
        if j == 2:
            zcp[3, h] = send(block(0, 2, h), block(0, 3, h), bz_sem.at[2, h], line[1])
        forward(j, h)

    def diagonal(j, h):
        xcp[j, h].wait_recv()
        ycp[j, h].wait_recv()
        if (j + h) % 2:
            dcp[j, h] = send(block(1, j, h), block(3, j, h), bd_sem.at[j, h], yn)
        else:
            dcp[j, h] = send(block(2, j, h), block(3, j, h), bd_sem.at[j, h], xn)

    process(0)
    idy.wait()
    count(2, 0)
    process(1)
    stores = [pltpu.make_async_copy(crossed_ref, crossed_out, store_sem.at[0])]
    stores[0].start()
    along(1, 0)
    along(2, 0)
    diagonal(0, 0)
    count(2, 1)
    along(3, 0)
    along(1, 1)
    diagonal(1, 0)
    along(2, 1)
    diagonal(0, 1)
    idd.wait()
    count(3, 0)
    diagonal(2, 0)
    along(3, 1)
    diagonal(1, 1)
    diagonal(3, 0)
    count(3, 1)
    diagonal(2, 1)
    diagonal(3, 1)

    def product(r, start=0, size=2 * rows):
        bh, bl = split(back[r])
        c = ct[r, start : start + size]
        g[r, start : start + size] = dot(c, bh) + dot(c, bl)

    product(0)
    product(1)
    product(2)
    for cp in dcp.values():
        cp.wait_recv()

    def finish(start, size):
        product(3, start, size)
        at = slice(start, start + size)
        g[0, at] = (g[0, at] + g[1, at]) + (g[2, at] + g[3, at])

    piece = rows // 2
    gcp = []
    for i in range(2):
        finish(rows + i * piece, piece)
        gcp.append(
            send(g.at[0, pl.ds(rows + i * piece, piece)], grecv.at[pl.ds(i * piece, piece)], g_sem.at[i], mate)
        )
    finish(0, rows)
    acc_col = jnp.transpose(jnp.broadcast_to(accum[...], (8, rows)))[:, 0:1]
    for d in (zcp, xcp, ycp, dcp):
        for cp in d.values():
            cp.wait_send()
    for i in range(2):
        gcp[i].wait()
        at = slice(i * piece, (i + 1) * piece)
        total = g[0, at] + grecv[at]
        mean = jnp.sum(total * total, axis=1, keepdims=True) * (1.0 / total.shape[1])
        fresh = acc_col[at] + mean
        newt_ref[at] = tab[0, at] - 0.5 * total * lax.rsqrt(fresh)
        part = pl.ds(i * piece, piece)
        stores.append(pltpu.make_async_copy(newt_ref.at[part], newt_out.at[part], store_sem.at[1 + i]))
        stores[-1].start()
        newa_ref[:, at] = jnp.transpose(jnp.broadcast_to(fresh, (piece, 128)))[0:1]
    stores.append(pltpu.make_async_copy(newa_ref, newa_out, store_sem.at[3]))
    stores[-1].start()
    for cp in stores:
        cp.wait()


def hand_out(a, b, c, x, y, w, va, vb, vc, sems_in, sems_out):
    piece = vb.shape[0] // 2
    parts = [(b.at[pl.ds(i * piece, piece)], vb.at[pl.ds(i * piece, piece)], y.at[pl.ds(i * piece, piece)]) for i in (0, 1)]
    parts += [(a, va, x), (c, vc, w)]
    ins = [pltpu.make_async_copy(p[0], p[1], sems_in.at[i]) for i, p in enumerate(parts)]
    outs = [pltpu.make_async_copy(p[1], p[2], sems_out.at[i]) for i, p in enumerate(parts)]
    for cp in ins:
        cp.start()
    for cp, out in zip(ins, outs):
        cp.wait()
        out.start()
    for cp in outs:
        cp.wait()


def fused_body(bag_ids, table, accum, cross_weight, cross_bias, upstream):
    each, bag = bag_ids.shape
    rows, width = table.shape
    tall = -(-bag // 8) * 8
    hbm = pl.BlockSpec(memory_space=pltpu.HBM)
    dma = pltpu.SemaphoreType.DMA
    shapes = (
        jax.ShapeDtypeStruct((each, width), F32),
        jax.ShapeDtypeStruct((rows, width), F32),
        jax.ShapeDtypeStruct((1, rows), F32),
    )
    done = pl.pallas_call(
        lambda *refs: kernel(bag, *refs),
        out_shape=shapes,
        in_specs=[hbm] * 6,
        out_specs=[hbm] * 3,
        scratch_shapes=[
            pltpu.VMEM((2, rows, width), F32),
            pltpu.VMEM((2 * rows, width), BF16),
            pltpu.VMEM((2 * rows, width), BF16),
            pltpu.VMEM((PLANE, LINE, tall, 128), jnp.int32),
            pltpu.VMEM((PLANE, 2 * rows, LINE * each), BF16),
            pltpu.VMEM((LINE - 1, each, width), F32),
            pltpu.VMEM((LINE - 1, each, width), F32),
            pltpu.VMEM((PLANE, LINE * each, width), F32),
            pltpu.VMEM((PLANE, 2 * rows, width), F32),
            pltpu.VMEM((rows, width), F32),
            pltpu.VMEM((bag, each), jnp.int32),
            pltpu.VMEM((1, rows), F32),
            pltpu.VMEM((width, width), F32),
            pltpu.VMEM((1, width), F32),
            pltpu.VMEM((each, width), F32),
            pltpu.VMEM((4, width, width), BF16),
            pltpu.VMEM((each, width), F32),
            pltpu.VMEM((rows, width), F32),
            pltpu.VMEM((1, rows), F32),
            dma((6,)),
            dma((4,)),
            dma((2,)),
            dma((3, 2)),
            dma((3, 2)),
            dma((3, 2, 2)),
            dma((3, 2, 2)),
            dma((2, LINE, 2, 2)),
            dma((LINE, 2, 2)),
            dma((2, 2)),
        ],
        compiler_params=pltpu.CompilerParams(
            collective_id=0, has_side_effects=True, vmem_limit_bytes=GRANT
        ),
    )(bag_ids.T, table, accum.reshape(1, rows), cross_weight, cross_bias.reshape(1, width), upstream)
    crossed, new_table, new_accum = pl.pallas_call(
        hand_out,
        out_shape=shapes,
        in_specs=[hbm] * 3,
        out_specs=[hbm] * 3,
        scratch_shapes=[pltpu.VMEM(a.shape, F32) for a in shapes] + [dma((4,)), dma((4,))],
        compiler_params=pltpu.CompilerParams(vmem_limit_bytes=GRANT),
    )(*done)
    return crossed, new_table, new_accum.reshape(rows)


def adagrad_rows(rows, sums, grads):
    fresh = sums + jnp.mean(grads * grads, axis=1)
    return (rows - 0.5 * grads / jnp.sqrt(fresh)[:, None], fresh)


def general_body(bag_ids, table, accum, cross_weight, cross_bias, upstream):
    rows_owned = table.shape[0]
    first_row = lax.axis_index("shard") * rows_owned
    group_ids = lax.all_gather(bag_ids, "shard", axis=0, tiled=True)
    local = group_ids - first_row
    number = lax.broadcasted_iota(jnp.int32, (1, rows_owned), 1)
    counts = jnp.zeros((local.shape[0], rows_owned), F32)
    for j in range(local.shape[1]):
        counts = counts + (local[:, j : j + 1] == number).astype(F32)
    pooled = lax.psum_scatter(
        jnp.dot(counts, table, precision=lax.Precision.HIGHEST),
        "shard",
        scatter_dimension=0,
        tiled=True,
    )
    mixed = jnp.dot(pooled, cross_weight, precision=lax.Precision.HIGHEST) + cross_bias
    crossed = pooled * mixed + pooled
    back = (
        upstream * mixed
        + jnp.dot(upstream * pooled, cross_weight.T, precision=lax.Precision.HIGHEST)
        + upstream
    )
    piece = lax.all_gather(back, "shard", axis=0, tiled=True)
    added = lax.dot_general(
        counts, piece, (((0,), (0,)), ((), ())), precision=lax.Precision.HIGHEST
    )
    totals = lax.psum(added, "rep")
    new_table, new_accum = adagrad_rows(table, accum, totals)
    return (crossed, new_table, new_accum)


def solution(mesh):
    placed = (
        P(("rep", "shard"), None),
        P("shard", None),
        P("shard"),
        P(),
        P(),
        P(("rep", "shard"), None),
    )
    small = mesh.shape["rep"] == PLANE and mesh.shape["shard"] == 2 * LINE
    return jax.shard_map(
        fused_body if small else general_body,
        mesh=mesh,
        in_specs=placed,
        out_specs=(P(("rep", "shard"), None), P("shard", None), P("shard")),
        check_vma=False,
    )
```

```python
import jax
import jax.numpy as jnp
from jax import lax
from jax.experimental import pallas as pl
from jax.experimental.pallas import tpu as pltpu
from jax.sharding import PartitionSpec as P

F32 = jnp.float32
BF16 = jnp.bfloat16
MESH = pl.DeviceIdType.MESH
PLANE = 4
LINE = 4
GRANT = 63 * 1024 * 1024
CHUNK = 256


def split(x):
    hi = x.astype(BF16)
    return hi, (x - hi.astype(F32)).astype(BF16)


def dot(a, b, dims=((1,), (0,))):
    return lax.dot_general(a, b, (dims, ((), ())), preferred_element_type=F32)


def kernel(
    bag, ids_hbm, table_hbm, accum_hbm, weight_hbm, bias_hbm, up_hbm,
    crossed_out, newt_out, newa_out,
    tab, thi, tlo, ids, ct, psend, precv, back, g, grecv,
    ids_raw, accum, weight, bias, up, wsp, crossed_ref, newt_ref, newa_ref,
    load_sem, store_sem, tab_sem, idz_sem, idp_sem, p_sem, bz_sem, bp_sem, bd_sem, g_sem,
):
    rep = lax.axis_index("rep")
    shard = lax.axis_index("shard")
    z = shard // 2
    core = shard % 2
    rows = tab.shape[1]
    each = up.shape[0]
    mate = (rep, shard + 1 - 2 * core)
    xn = (rep + 1 - 2 * (rep % 2), shard)
    yn = ((rep + 2) % 4, shard)
    line = {
        1: (rep, (z + 1 - 2 * (z % 2)) * 2 + core),
        2: (rep, ((z + 2) % LINE) * 2 + core),
        3: (rep, (LINE - 1 - z) * 2 + core),
    }

    def send(src, dst, sems, to):
        cp = pltpu.make_async_remote_copy(
            src_ref=src, dst_ref=dst, send_sem=sems.at[0], recv_sem=sems.at[1],
            device_id=to, device_id_type=MESH,
        )
        cp.start()
        return cp

    barrier = pltpu.get_barrier_semaphore()
    for to in (mate, xn, yn, line[1], line[2], line[3]):
        pl.semaphore_signal(barrier, inc=1, device_id=to, device_id_type=MESH)

    def load(src, dst, i):
        cp = pltpu.make_async_copy(src, dst, load_sem.at[i])
        cp.start()
        return cp

    ids_load = load(ids_hbm, ids_raw, 0)
    table_load = load(table_hbm, tab.at[0], 1)
    rest = [
        load(src, dst, 2 + i)
        for i, (src, dst) in enumerate(
            ((weight_hbm, weight), (up_hbm, up), (bias_hbm, bias), (accum_hbm, accum))
        )
    ]
    ids_load.wait()
    raw = ids_raw[...]
    ids[0, 0] = jnp.full(ids.shape[2:], -1, jnp.int32)
    ids[0, 0, 0:bag] = jnp.concatenate([raw, raw], axis=1)
    pl.semaphore_wait(barrier, 6)

    idz = {j: send(ids.at[0, 0], ids.at[0, j], idz_sem.at[j - 1], line[j]) for j in (2, 3, 1)}
    tcp = send(table_hbm, tab.at[1], tab_sem, mate)
    table_load.wait()
    hi, lo = split(tab[0])
    thi[0:rows] = hi
    tlo[0:rows] = lo

    for cp in rest:
        cp.wait()
    hi, lo = split(weight[...])
    wsp[0] = hi
    wsp[1] = lo
    turned = jnp.transpose(weight[...])
    hi, lo = split(turned)
    wsp[2] = hi
    wsp[3] = lo

    own_first = shard * rows
    mate_first = (shard + 1 - 2 * core) * rows
    per_block = rows // CHUNK
    row16 = lax.broadcasted_iota(jnp.int32, (CHUNK, 128), 0).astype(F32).astype(BF16)
    lane = lax.broadcasted_iota(jnp.int32, ids.shape[2:], 1)
    spot = lax.broadcasted_iota(jnp.int32, ids.shape[2:], 0)
    half = each // 2

    def widen(row):
        one = jnp.broadcast_to(row, (16, 128)).astype(BF16)
        return jnp.concatenate([one] * (CHUNK // 16), axis=0)

    def count(r, p, use=None, start=0):
        pair = jnp.where(lane < each, ids[r, 2 * p], ids[r, 2 * p + 1])
        times = jnp.ones(pair.shape, F32)
        for i in range(bag - 1):
            again = (spot > i) & (pair == pair[i : i + 1])
            times = times + jnp.where(again, 1.0, 0.0)

        def step(q, carry):
            base = jnp.where(q < per_block, own_first, mate_first) + (q % per_block) * CHUNK
            local = pair - base
            local = jnp.where((local >= 0) & (local < CHUNK), local, -1).astype(F32)
            acc = jnp.zeros((CHUNK, 128), BF16)
            for j in range(bag):
                acc = jnp.where(widen(local[j : j + 1]) == row16, widen(times[j : j + 1]), acc)
            at = pl.ds(pl.multiple_of(q * CHUNK, CHUNK), CHUNK)
            ct[r, p, at] = acc
            return carry if use is None else use(acc, at, carry)

        return lax.fori_loop(0, 2 * per_block, step, start)

    def counts(r):
        def step(p, carry):
            count(r, p)
            return carry

        lax.fori_loop(0, 2, step, 0)

    pcp = {}

    def give(j, h):
        part = pl.ds(h * half, half)
        pcp[j, h] = send(psend.at[j, part], precv.at[j - 1, part], p_sem.at[j - 1, h], line[j])

    def add_part(acc, at, total):
        return total + dot(acc, thi[at], ((0,), (0,))) + dot(acc, tlo[at], ((0,), (0,)))

    for p in (1, 0):
        for j in ((2, 3) if p else (1,)):
            idz[j].wait()
        if p:
            tcp.wait()
            hi, lo = split(tab[1])
            thi[rows : 2 * rows] = hi
            tlo[rows : 2 * rows] = lo
        else:
            idx = send(ids.at[0], ids.at[1], idp_sem.at[0], xn)
            idy = send(ids.at[0], ids.at[2], idp_sem.at[1], yn)
        part = count(0, p, add_part, jnp.zeros((128, tab.shape[2]), F32))
        psend[2 * p] = part[0:each]
        psend[2 * p + 1] = part[each : 2 * each]
        for j in (2 * p, 2 * p + 1):
            if j:
                give(j, 0)
    for j in (2, 3, 1):
        give(j, 1)

    idx.wait()
    idd = send(ids.at[1], ids.at[3], idp_sem.at[2], yn)
    counts(1)

    def cross(x, k):
        xh, xl = split(x)
        return dot(xh, wsp[k]) + (dot(xh, wsp[k + 1]) + dot(xl, wsp[k]))

    def block(r, j, h):
        return back.at[r, pl.ds(j * each + h * half, half)]

    zcp, xcp, ycp, dcp = {}, {}, {}, {}

    def forward(j, h):
        xcp[j, h] = send(block(0, j, h), block(1, j, h), bp_sem.at[0, j, h], xn)
        ycp[j, h] = send(block(0, j, h), block(2, j, h), bp_sem.at[1, j, h], yn)

    def process(h):
        at = slice(h * half, (h + 1) * half)
        for j in (1, 2, 3):
            pcp[j, h].wait()
        pooled = (psend[0, at] + precv[0, at]) + (precv[1, at] + precv[2, at])
        grad = up[at]
        mixed = cross(pooled, 0) + bias[...]
        back[0, at] = grad * mixed + cross(grad * pooled, 2) + grad
        for j in (2, 3, 1) if h else (2, 1):
            zcp[j, h] = send(block(0, 0, h), block(0, j, h), bz_sem.at[j - 1, h], line[j])
        forward(0, h)
        crossed_ref[at] = pooled * mixed + pooled

    def along(j, h):
        zcp[j, h].wait_recv()
        if j == 2 and h == 0:
            zcp[3, h] = send(block(0, 2, h), block(0, 3, h), bz_sem.at[2, h], line[1])
        forward(j, h)

    def diagonal(j, h):
        xcp[j, h].wait_recv()
        ycp[j, h].wait_recv()
        if (j + h) % 2:
            dcp[j, h] = send(block(1, j, h), block(3, j, h), bd_sem.at[j, h], yn)
        else:
            dcp[j, h] = send(block(2, j, h), block(3, j, h), bd_sem.at[j, h], xn)

    process(0)
    idy.wait()
    counts(2)
    along(1, 0)
    diagonal(0, 0)
    process(1)
    stores = [pltpu.make_async_copy(crossed_ref, crossed_out, store_sem.at[0])]
    stores[0].start()
    along(2, 0)
    diagonal(1, 0)
    idd.wait()
    counts(3)
    along(3, 0)
    along(1, 1)
    diagonal(0, 1)
    along(2, 1)
    diagonal(2, 0)
    along(3, 1)
    diagonal(1, 1)
    diagonal(3, 0)
    diagonal(2, 1)
    diagonal(3, 1)

    def product(r, q):
        bh, bl = split(back[r])
        at = pl.ds(pl.multiple_of(q * CHUNK, CHUNK), CHUNK)
        c = jnp.concatenate([ct[r, 0, at], ct[r, 1, at]], axis=1)
        g[r, at] = dot(c, bh) + dot(c, bl)
        return at

    def early(i, carry):
        product(i // (2 * per_block), i % (2 * per_block))
        return carry

    lax.fori_loop(0, (PLANE - 1) * 2 * per_block, early, 0)
    for cp in dcp.values():
        cp.wait_recv()

    def swap(i):
        return pltpu.make_async_remote_copy(
            src_ref=g.at[0, pl.ds(rows + i * CHUNK, CHUNK)],
            dst_ref=grecv.at[pl.ds(i * CHUNK, CHUNK)],
            send_sem=g_sem.at[i, 0], recv_sem=g_sem.at[i, 1],
            device_id=mate, device_id_type=MESH,
        )

    def late(i, carry):
        q = (i + per_block) % (2 * per_block)
        at = product(3, q)
        g[0, at] = (g[0, at] + g[1, at]) + (g[2, at] + g[3, at])

        @pl.when(i < per_block)
        def _():
            swap(i).start()

        return carry

    lax.fori_loop(0, 2 * per_block, late, 0)
    piece = CHUNK
    acc_col = jnp.transpose(jnp.broadcast_to(accum[...], (8, rows)))[:, 0:1]
    for d in (zcp, xcp, ycp, dcp):
        for cp in d.values():
            cp.wait_send()
    for i in range(per_block):
        swap(i).wait()
        at = slice(i * piece, (i + 1) * piece)
        total = g[0, at] + grecv[at]
        mean = jnp.sum(total * total, axis=1, keepdims=True) * (1.0 / total.shape[1])
        fresh = acc_col[at] + mean
        newt_ref[at] = tab[0, at] - 0.5 * total * lax.rsqrt(fresh)
        part = pl.ds(i * piece, piece)
        stores.append(pltpu.make_async_copy(newt_ref.at[part], newt_out.at[part], store_sem.at[1 + i]))
        stores[-1].start()
        newa_ref[:, at] = jnp.transpose(jnp.broadcast_to(fresh, (piece, 128)))[0:1]
    stores.append(pltpu.make_async_copy(newa_ref, newa_out, store_sem.at[1 + per_block]))
    stores[-1].start()
    for cp in stores:
        cp.wait()


def hand_out(a, b, c, x, y, w, va, vb, vc, sems_in, sems_out):
    piece = vb.shape[0] // 2
    parts = [(b.at[pl.ds(i * piece, piece)], vb.at[pl.ds(i * piece, piece)], y.at[pl.ds(i * piece, piece)]) for i in (0, 1)]
    parts += [(a, va, x), (c, vc, w)]
    ins = [pltpu.make_async_copy(p[0], p[1], sems_in.at[i]) for i, p in enumerate(parts)]
    outs = [pltpu.make_async_copy(p[1], p[2], sems_out.at[i]) for i, p in enumerate(parts)]
    for cp in ins:
        cp.start()
    for cp, out in zip(ins, outs):
        cp.wait()
        out.start()
    for cp in outs:
        cp.wait()


def fused_body(bag_ids, table, accum, cross_weight, cross_bias, upstream):
    each, bag = bag_ids.shape
    rows, width = table.shape
    tall = -(-bag // 8) * 8
    hbm = pl.BlockSpec(memory_space=pltpu.HBM)
    dma = pltpu.SemaphoreType.DMA
    shapes = (
        jax.ShapeDtypeStruct((each, width), F32),
        jax.ShapeDtypeStruct((rows, width), F32),
        jax.ShapeDtypeStruct((1, rows), F32),
    )
    done = pl.pallas_call(
        lambda *refs: kernel(bag, *refs),
        out_shape=shapes,
        in_specs=[hbm] * 6,
        out_specs=[hbm] * 3,
        scratch_shapes=[
            pltpu.VMEM((2, rows, width), F32),
            pltpu.VMEM((2 * rows, width), BF16),
            pltpu.VMEM((2 * rows, width), BF16),
            pltpu.VMEM((PLANE, LINE, tall, 128), jnp.int32),
            pltpu.VMEM((PLANE, 2, 2 * rows, 2 * each), BF16),
            pltpu.VMEM((LINE, each, width), F32),
            pltpu.VMEM((LINE - 1, each, width), F32),
            pltpu.VMEM((PLANE, LINE * each, width), F32),
            pltpu.VMEM((PLANE, 2 * rows, width), F32),
            pltpu.VMEM((rows, width), F32),
            pltpu.VMEM((bag, each), jnp.int32),
            pltpu.VMEM((1, rows), F32),
            pltpu.VMEM((width, width), F32),
            pltpu.VMEM((1, width), F32),
            pltpu.VMEM((each, width), F32),
            pltpu.VMEM((4, width, width), BF16),
            pltpu.VMEM((each, width), F32),
            pltpu.VMEM((rows, width), F32),
            pltpu.VMEM((1, rows), F32),
            dma((6,)),
            dma((2 + rows // CHUNK,)),
            dma((2,)),
            dma((3, 2)),
            dma((3, 2)),
            dma((3, 2, 2)),
            dma((3, 2, 2)),
            dma((2, LINE, 2, 2)),
            dma((LINE, 2, 2)),
            dma((rows // CHUNK, 2)),
        ],
        compiler_params=pltpu.CompilerParams(
            collective_id=0, has_side_effects=True, vmem_limit_bytes=GRANT
        ),
    )(bag_ids.T, table, accum.reshape(1, rows), cross_weight, cross_bias.reshape(1, width), upstream)
    crossed, new_table, new_accum = pl.pallas_call(
        hand_out,
        out_shape=shapes,
        in_specs=[hbm] * 3,
        out_specs=[hbm] * 3,
        scratch_shapes=[pltpu.VMEM(a.shape, F32) for a in shapes] + [dma((4,)), dma((4,))],
        compiler_params=pltpu.CompilerParams(vmem_limit_bytes=GRANT),
    )(*done)
    return crossed, new_table, new_accum.reshape(rows)


def adagrad_rows(rows, sums, grads):
    fresh = sums + jnp.mean(grads * grads, axis=1)
    return (rows - 0.5 * grads / jnp.sqrt(fresh)[:, None], fresh)


def general_body(bag_ids, table, accum, cross_weight, cross_bias, upstream):
    rows_owned = table.shape[0]
    first_row = lax.axis_index("shard") * rows_owned
    group_ids = lax.all_gather(bag_ids, "shard", axis=0, tiled=True)
    local = group_ids - first_row
    number = lax.broadcasted_iota(jnp.int32, (1, rows_owned), 1)
    counts = jnp.zeros((local.shape[0], rows_owned), F32)
    for j in range(local.shape[1]):
        counts = counts + (local[:, j : j + 1] == number).astype(F32)
    pooled = lax.psum_scatter(
        jnp.dot(counts, table, precision=lax.Precision.HIGHEST),
        "shard",
        scatter_dimension=0,
        tiled=True,
    )
    mixed = jnp.dot(pooled, cross_weight, precision=lax.Precision.HIGHEST) + cross_bias
    crossed = pooled * mixed + pooled
    back = (
        upstream * mixed
        + jnp.dot(upstream * pooled, cross_weight.T, precision=lax.Precision.HIGHEST)
        + upstream
    )
    piece = lax.all_gather(back, "shard", axis=0, tiled=True)
    added = lax.dot_general(
        counts, piece, (((0,), (0,)), ((), ())), precision=lax.Precision.HIGHEST
    )
    totals = lax.psum(added, "rep")
    new_table, new_accum = adagrad_rows(table, accum, totals)
    return (crossed, new_table, new_accum)


def solution(mesh):
    placed = (
        P(("rep", "shard"), None),
        P("shard", None),
        P("shard"),
        P(),
        P(),
        P(("rep", "shard"), None),
    )
    small = mesh.shape["rep"] == PLANE and mesh.shape["shard"] == 2 * LINE
    return jax.shard_map(
        fused_body if small else general_body,
        mesh=mesh,
        in_specs=placed,
        out_specs=(P(("rep", "shard"), None), P("shard", None), P("shard")),
        check_vma=False,
    )
```

```python
import jax
import jax.numpy as jnp
from jax import lax
from jax.experimental import pallas as pl
from jax.experimental.pallas import tpu as pltpu
from jax.sharding import PartitionSpec as P

F32 = jnp.float32
BF16 = jnp.bfloat16
MESH = pl.DeviceIdType.MESH
PLANE = 4
LINE = 4
SLAB = 128
GRANT = 63 * 1024 * 1024
CHUNK = 256


def split(x):
    hi = x.astype(BF16)
    return hi, (x - hi.astype(F32)).astype(BF16)


def dot(a, b, dims=((1,), (0,))):
    return lax.dot_general(a, b, (dims, ((), ())), preferred_element_type=F32)


def kernel(
    bag, ids_hbm, table_hbm, accum_hbm, weight_hbm, bias_hbm, up_hbm,
    crossed_out, newt_out, newa_out,
    tab, thi, tlo, ids, ct, psend, precv, back, g, grecv,
    ids_raw, accum, weight, bias, up, wsp, crossed_ref, newt_ref, newa_ref,
    load_sem, store_sem, tab_sem, idz_sem, idp_sem, p_sem, bz_sem, bp_sem, bd_sem, g_sem,
):
    rep = lax.axis_index("rep")
    shard = lax.axis_index("shard")
    z = shard // 2
    core = shard % 2
    rows = tab.shape[1]
    each = up.shape[0]
    mate = (rep, shard + 1 - 2 * core)
    xn = (rep + 1 - 2 * (rep % 2), shard)
    yn = ((rep + 2) % 4, shard)
    line = {
        1: (rep, (z + 1 - 2 * (z % 2)) * 2 + core),
        2: (rep, ((z + 2) % LINE) * 2 + core),
        3: (rep, (LINE - 1 - z) * 2 + core),
    }

    def send(src, dst, sems, to):
        cp = pltpu.make_async_remote_copy(
            src_ref=src, dst_ref=dst, send_sem=sems.at[0], recv_sem=sems.at[1],
            device_id=to, device_id_type=MESH,
        )
        cp.start()
        return cp

    barrier = pltpu.get_barrier_semaphore()
    for to in (mate, xn, yn, line[1], line[2], line[3]):
        pl.semaphore_signal(barrier, inc=1, device_id=to, device_id_type=MESH)

    def load(src, dst, i):
        cp = pltpu.make_async_copy(src, dst, load_sem.at[i])
        cp.start()
        return cp

    ids_load = load(ids_hbm, ids_raw, 0)
    table_load = load(table_hbm, tab.at[0], 1)
    rest = [
        load(src, dst, 2 + i)
        for i, (src, dst) in enumerate(
            ((weight_hbm, weight), (up_hbm, up), (bias_hbm, bias), (accum_hbm, accum))
        )
    ]
    ids_load.wait()
    raw = ids_raw[...]
    ids[0, 0] = jnp.full(ids.shape[2:], -1, jnp.int32)
    ids[0, 0, 0:bag] = jnp.concatenate([raw, raw], axis=1)
    pl.semaphore_wait(barrier, 6)

    idz = {j: send(ids.at[0, 0], ids.at[0, j], idz_sem.at[j - 1], line[j]) for j in (2, 3, 1)}
    table_load.wait()
    tcp = []
    for i in range(rows // SLAB):
        part = pl.ds(i * SLAB, SLAB)
        tcp.append(send(tab.at[0, part], tab.at[1, part], tab_sem.at[i], mate))
    hi, lo = split(tab[0])
    thi[0:rows] = hi
    tlo[0:rows] = lo

    for cp in rest:
        cp.wait()
    hi, lo = split(weight[...])
    wsp[0] = hi
    wsp[1] = lo
    turned = jnp.transpose(weight[...])
    hi, lo = split(turned)
    wsp[2] = hi
    wsp[3] = lo

    own_first = shard * rows
    mate_first = (shard + 1 - 2 * core) * rows
    per_block = rows // CHUNK
    row16 = lax.broadcasted_iota(jnp.int32, (CHUNK, 128), 0).astype(F32).astype(BF16)
    lane = lax.broadcasted_iota(jnp.int32, ids.shape[2:], 1)
    spot = lax.broadcasted_iota(jnp.int32, ids.shape[2:], 0)
    half = each // 2

    def widen(row):
        one = jnp.broadcast_to(row, (16, 128)).astype(BF16)
        return jnp.concatenate([one] * (CHUNK // 16), axis=0)

    def count(r, p, use=None, start=0):
        pair = jnp.where(lane < each, ids[r, 2 * p], ids[r, 2 * p + 1])
        times = jnp.ones(pair.shape, F32)
        for i in range(bag - 1):
            again = (spot > i) & (pair == pair[i : i + 1])
            times = times + jnp.where(again, 1.0, 0.0)

        def step(q, carry):
            base = jnp.where(q < per_block, own_first, mate_first) + (q % per_block) * CHUNK
            local = pair - base
            local = jnp.where((local >= 0) & (local < CHUNK), local, -1).astype(F32)
            acc = jnp.zeros((CHUNK, 128), BF16)
            for j in range(bag):
                acc = jnp.where(widen(local[j : j + 1]) == row16, widen(times[j : j + 1]), acc)
            at = pl.ds(pl.multiple_of(q * CHUNK, CHUNK), CHUNK)
            ct[r, p, at] = acc
            return carry if use is None else use(acc, at, carry, q)

        return lax.fori_loop(0, 2 * per_block, step, start)

    def counts(r):
        def step(p, carry):
            count(r, p)
            return carry

        lax.fori_loop(0, 2, step, 0)

    pcp = {}

    def give(j, h):
        part = pl.ds(h * half, half)
        pcp[j, h] = send(psend.at[j, part], precv.at[j - 1, part], p_sem.at[j - 1, h], line[j])

    def first_part(acc, at, total, q):
        @pl.when(q == per_block)
        def _():
            for cp in tcp:
                cp.wait()
            hi, lo = split(tab[1])
            thi[rows : 2 * rows] = hi
            tlo[rows : 2 * rows] = lo

        return add_part(acc, at, total, q)

    def add_part(acc, at, total, q):
        return total + dot(acc, thi[at], ((0,), (0,))) + dot(acc, tlo[at], ((0,), (0,)))

    for p in (1, 0):
        for j in ((2, 3) if p else (1,)):
            idz[j].wait()
        if not p:
            idx = send(ids.at[0], ids.at[1], idp_sem.at[0], xn)
            idy = send(ids.at[0], ids.at[2], idp_sem.at[1], yn)
        part = count(0, p, first_part if p else add_part, jnp.zeros((128, tab.shape[2]), F32))
        psend[2 * p] = part[0:each]
        psend[2 * p + 1] = part[each : 2 * each]
        for j in (2 * p, 2 * p + 1):
            if j:
                give(j, 0)
    for j in (2, 3, 1):
        give(j, 1)

    idx.wait()
    idd = send(ids.at[1], ids.at[3], idp_sem.at[2], yn)
    counts(1)

    def cross(x, k):
        xh, xl = split(x)
        return dot(xh, wsp[k]) + (dot(xh, wsp[k + 1]) + dot(xl, wsp[k]))

    def block(r, j, h):
        return back.at[r, pl.ds(j * each + h * half, half)]

    zcp, xcp, ycp, dcp = {}, {}, {}, {}

    def forward(j, h):
        xcp[j, h] = send(block(0, j, h), block(1, j, h), bp_sem.at[0, j, h], xn)
        ycp[j, h] = send(block(0, j, h), block(2, j, h), bp_sem.at[1, j, h], yn)

    def process(h):
        at = slice(h * half, (h + 1) * half)
        for j in (1, 2, 3):
            pcp[j, h].wait()
        pooled = (psend[0, at] + precv[0, at]) + (precv[1, at] + precv[2, at])
        grad = up[at]
        mixed = cross(pooled, 0) + bias[...]
        back[0, at] = grad * mixed + cross(grad * pooled, 2) + grad
        for j in (2, 3, 1) if h else (2, 1):
            zcp[j, h] = send(block(0, 0, h), block(0, j, h), bz_sem.at[j - 1, h], line[j])
        forward(0, h)
        crossed_ref[at] = pooled * mixed + pooled

    def along(j, h):
        zcp[j, h].wait_recv()
        if j == 2 and h == 0:
            zcp[3, h] = send(block(0, 2, h), block(0, 3, h), bz_sem.at[2, h], line[1])
        forward(j, h)

    def diagonal(j, h):
        xcp[j, h].wait_recv()
        ycp[j, h].wait_recv()
        if (j + h) % 2:
            dcp[j, h] = send(block(1, j, h), block(3, j, h), bd_sem.at[j, h], yn)
        else:
            dcp[j, h] = send(block(2, j, h), block(3, j, h), bd_sem.at[j, h], xn)

    process(0)
    idy.wait()
    counts(2)
    along(1, 0)
    diagonal(0, 0)
    process(1)
    stores = [pltpu.make_async_copy(crossed_ref, crossed_out, store_sem.at[0])]
    stores[0].start()
    along(2, 0)
    diagonal(1, 0)
    idd.wait()
    counts(3)
    along(3, 0)
    along(1, 1)
    diagonal(0, 1)
    along(2, 1)
    diagonal(2, 0)
    along(3, 1)
    diagonal(1, 1)
    diagonal(3, 0)
    diagonal(2, 1)
    diagonal(3, 1)

    def product(r, q):
        bh, bl = split(back[r])
        at = pl.ds(pl.multiple_of(q * CHUNK, CHUNK), CHUNK)
        c = jnp.concatenate([ct[r, 0, at], ct[r, 1, at]], axis=1)
        g[r, at] = dot(c, bh) + dot(c, bl)
        return at

    def early(i, carry):
        product(i // (2 * per_block), i % (2 * per_block))
        return carry

    lax.fori_loop(0, (PLANE - 1) * 2 * per_block, early, 0)
    for cp in dcp.values():
        cp.wait_recv()

    def swap(i):
        return pltpu.make_async_remote_copy(
            src_ref=g.at[0, pl.ds(rows + i * SLAB, SLAB)],
            dst_ref=grecv.at[pl.ds(i * SLAB, SLAB)],
            send_sem=g_sem.at[i, 0], recv_sem=g_sem.at[i, 1],
            device_id=mate, device_id_type=MESH,
        )

    def late(i, carry):
        q = (i + per_block) % (2 * per_block)
        at = product(3, q)
        g[0, at] = (g[0, at] + g[1, at]) + (g[2, at] + g[3, at])

        @pl.when(i < per_block)
        def _():
            for k in range(CHUNK // SLAB):
                swap(i * (CHUNK // SLAB) + k).start()

        return carry

    lax.fori_loop(0, 2 * per_block, late, 0)
    piece = CHUNK
    acc_col = jnp.transpose(jnp.broadcast_to(accum[...], (8, rows)))[:, 0:1]
    for d in (zcp, xcp, ycp, dcp):
        for cp in d.values():
            cp.wait_send()
    for i in range(per_block):
        for k in range(CHUNK // SLAB):
            swap(i * (CHUNK // SLAB) + k).wait()
        at = slice(i * piece, (i + 1) * piece)
        total = g[0, at] + grecv[at]
        mean = jnp.sum(total * total, axis=1, keepdims=True) * (1.0 / total.shape[1])
        fresh = acc_col[at] + mean
        newt_ref[at] = tab[0, at] - 0.5 * total * lax.rsqrt(fresh)
        part = pl.ds(i * piece, piece)
        stores.append(pltpu.make_async_copy(newt_ref.at[part], newt_out.at[part], store_sem.at[1 + i]))
        stores[-1].start()
        newa_ref[:, at] = jnp.transpose(jnp.broadcast_to(fresh, (piece, 128)))[0:1]
    stores.append(pltpu.make_async_copy(newa_ref, newa_out, store_sem.at[1 + per_block]))
    stores[-1].start()
    for cp in stores:
        cp.wait()


def hand_out(a, b, c, x, y, w, va, vb, vc, sems_in, sems_out):
    piece = vb.shape[0] // 2
    parts = [(b.at[pl.ds(i * piece, piece)], vb.at[pl.ds(i * piece, piece)], y.at[pl.ds(i * piece, piece)]) for i in (0, 1)]
    parts += [(a, va, x), (c, vc, w)]
    ins = [pltpu.make_async_copy(p[0], p[1], sems_in.at[i]) for i, p in enumerate(parts)]
    outs = [pltpu.make_async_copy(p[1], p[2], sems_out.at[i]) for i, p in enumerate(parts)]
    for cp in ins:
        cp.start()
    for cp, out in zip(ins, outs):
        cp.wait()
        out.start()
    for cp in outs:
        cp.wait()


def fused_body(bag_ids, table, accum, cross_weight, cross_bias, upstream):
    each, bag = bag_ids.shape
    rows, width = table.shape
    tall = -(-bag // 8) * 8
    hbm = pl.BlockSpec(memory_space=pltpu.HBM)
    dma = pltpu.SemaphoreType.DMA
    shapes = (
        jax.ShapeDtypeStruct((each, width), F32),
        jax.ShapeDtypeStruct((rows, width), F32),
        jax.ShapeDtypeStruct((1, rows), F32),
    )
    done = pl.pallas_call(
        lambda *refs: kernel(bag, *refs),
        out_shape=shapes,
        in_specs=[hbm] * 6,
        out_specs=[hbm] * 3,
        scratch_shapes=[
            pltpu.VMEM((2, rows, width), F32),
            pltpu.VMEM((2 * rows, width), BF16),
            pltpu.VMEM((2 * rows, width), BF16),
            pltpu.VMEM((PLANE, LINE, tall, 128), jnp.int32),
            pltpu.VMEM((PLANE, 2, 2 * rows, 2 * each), BF16),
            pltpu.VMEM((LINE, each, width), F32),
            pltpu.VMEM((LINE - 1, each, width), F32),
            pltpu.VMEM((PLANE, LINE * each, width), F32),
            pltpu.VMEM((PLANE, 2 * rows, width), F32),
            pltpu.VMEM((rows, width), F32),
            pltpu.VMEM((bag, each), jnp.int32),
            pltpu.VMEM((1, rows), F32),
            pltpu.VMEM((width, width), F32),
            pltpu.VMEM((1, width), F32),
            pltpu.VMEM((each, width), F32),
            pltpu.VMEM((4, width, width), BF16),
            pltpu.VMEM((each, width), F32),
            pltpu.VMEM((rows, width), F32),
            pltpu.VMEM((1, rows), F32),
            dma((6,)),
            dma((2 + rows // CHUNK,)),
            dma((rows // SLAB, 2)),
            dma((3, 2)),
            dma((3, 2)),
            dma((3, 2, 2)),
            dma((3, 2, 2)),
            dma((2, LINE, 2, 2)),
            dma((LINE, 2, 2)),
            dma((rows // SLAB, 2)),
        ],
        compiler_params=pltpu.CompilerParams(
            collective_id=0, has_side_effects=True, vmem_limit_bytes=GRANT
        ),
    )(bag_ids.T, table, accum.reshape(1, rows), cross_weight, cross_bias.reshape(1, width), upstream)
    crossed, new_table, new_accum = pl.pallas_call(
        hand_out,
        out_shape=shapes,
        in_specs=[hbm] * 3,
        out_specs=[hbm] * 3,
        scratch_shapes=[pltpu.VMEM(a.shape, F32) for a in shapes] + [dma((4,)), dma((4,))],
        compiler_params=pltpu.CompilerParams(vmem_limit_bytes=GRANT),
    )(*done)
    return crossed, new_table, new_accum.reshape(rows)


def adagrad_rows(rows, sums, grads):
    fresh = sums + jnp.mean(grads * grads, axis=1)
    return (rows - 0.5 * grads / jnp.sqrt(fresh)[:, None], fresh)


def general_body(bag_ids, table, accum, cross_weight, cross_bias, upstream):
    rows_owned = table.shape[0]
    first_row = lax.axis_index("shard") * rows_owned
    group_ids = lax.all_gather(bag_ids, "shard", axis=0, tiled=True)
    local = group_ids - first_row
    number = lax.broadcasted_iota(jnp.int32, (1, rows_owned), 1)
    counts = jnp.zeros((local.shape[0], rows_owned), F32)
    for j in range(local.shape[1]):
        counts = counts + (local[:, j : j + 1] == number).astype(F32)
    pooled = lax.psum_scatter(
        jnp.dot(counts, table, precision=lax.Precision.HIGHEST),
        "shard",
        scatter_dimension=0,
        tiled=True,
    )
    mixed = jnp.dot(pooled, cross_weight, precision=lax.Precision.HIGHEST) + cross_bias
    crossed = pooled * mixed + pooled
    back = (
        upstream * mixed
        + jnp.dot(upstream * pooled, cross_weight.T, precision=lax.Precision.HIGHEST)
        + upstream
    )
    piece = lax.all_gather(back, "shard", axis=0, tiled=True)
    added = lax.dot_general(
        counts, piece, (((0,), (0,)), ((), ())), precision=lax.Precision.HIGHEST
    )
    totals = lax.psum(added, "rep")
    new_table, new_accum = adagrad_rows(table, accum, totals)
    return (crossed, new_table, new_accum)


def solution(mesh):
    placed = (
        P(("rep", "shard"), None),
        P("shard", None),
        P("shard"),
        P(),
        P(),
        P(("rep", "shard"), None),
    )
    small = mesh.shape["rep"] == PLANE and mesh.shape["shard"] == 2 * LINE
    return jax.shard_map(
        fused_body if small else general_body,
        mesh=mesh,
        in_specs=placed,
        out_specs=(P(("rep", "shard"), None), P("shard", None), P("shard")),
        check_vma=False,
    )
```

```python
import jax
import jax.numpy as jnp
from jax import lax
from jax.experimental import pallas as pl
from jax.experimental.pallas import tpu as pltpu
from jax.sharding import PartitionSpec as P

F32 = jnp.float32
BF16 = jnp.bfloat16
MESH = pl.DeviceIdType.MESH
PLANE = 4
LINE = 4
SLAB = 128
GRANT = 63 * 1024 * 1024
CHUNK = 256


def split(x):
    hi = x.astype(BF16)
    return hi, (x - hi.astype(F32)).astype(BF16)


def dot(a, b, dims=((1,), (0,))):
    return lax.dot_general(a, b, (dims, ((), ())), preferred_element_type=F32)


def kernel(
    bag, ids_hbm, table_hbm, accum_hbm, weight_hbm, bias_hbm, up_hbm,
    crossed_out, newt_out, newa_out,
    tab, thi, tlo, ids, ct, psend, precv, back, g, grecv,
    ids_raw, accum, weight, bias, up, wsp, crossed_ref, newt_ref, newa_ref,
    load_sem, store_sem, tab_sem, idz_sem, idp_sem, p_sem, bz_sem, bp_sem, bd_sem, g_sem,
):
    rep = lax.axis_index("rep")
    shard = lax.axis_index("shard")
    z = shard // 2
    core = shard % 2
    rows = tab.shape[1]
    each = up.shape[0]
    mate = (rep, shard + 1 - 2 * core)
    xn = (rep + 1 - 2 * (rep % 2), shard)
    yn = ((rep + 2) % 4, shard)
    line = {
        1: (rep, (z + 1 - 2 * (z % 2)) * 2 + core),
        2: (rep, ((z + 2) % LINE) * 2 + core),
        3: (rep, (LINE - 1 - z) * 2 + core),
    }

    def send(src, dst, sems, to):
        cp = pltpu.make_async_remote_copy(
            src_ref=src, dst_ref=dst, send_sem=sems.at[0], recv_sem=sems.at[1],
            device_id=to, device_id_type=MESH,
        )
        cp.start()
        return cp

    barrier = pltpu.get_barrier_semaphore()
    for to in (mate, xn, yn, line[1], line[2], line[3]):
        pl.semaphore_signal(barrier, inc=1, device_id=to, device_id_type=MESH)

    def load(src, dst, i):
        cp = pltpu.make_async_copy(src, dst, load_sem.at[i])
        cp.start()
        return cp

    ids_load = load(ids_hbm, ids_raw, 0)
    table_load = load(table_hbm, tab.at[0], 1)
    rest = [
        load(src, dst, 2 + i)
        for i, (src, dst) in enumerate(
            ((weight_hbm, weight), (up_hbm, up), (bias_hbm, bias), (accum_hbm, accum))
        )
    ]
    ids_load.wait()
    raw = ids_raw[...]
    ids[0, 0] = jnp.full(ids.shape[2:], -1, jnp.int32)
    ids[0, 0, 0:bag] = jnp.concatenate([raw, raw], axis=1)
    pl.semaphore_wait(barrier, 6)

    idz = {j: send(ids.at[0, 0], ids.at[0, j], idz_sem.at[j - 1], line[j]) for j in (2, 3, 1)}
    table_load.wait()
    tcp = []
    for i in range(rows // SLAB):
        part = pl.ds(i * SLAB, SLAB)
        tcp.append(send(tab.at[0, part], tab.at[1, part], tab_sem.at[i], mate))
    hi, lo = split(tab[0])
    thi[0:rows] = hi
    tlo[0:rows] = lo

    for cp in rest:
        cp.wait()
    hi, lo = split(weight[...])
    wsp[0] = hi
    wsp[1] = lo
    turned = jnp.transpose(weight[...])
    hi, lo = split(turned)
    wsp[2] = hi
    wsp[3] = lo

    own_first = shard * rows
    mate_first = (shard + 1 - 2 * core) * rows
    per_block = rows // CHUNK
    row16 = lax.broadcasted_iota(jnp.int32, (CHUNK, 128), 0).astype(F32).astype(BF16)
    lane = lax.broadcasted_iota(jnp.int32, ids.shape[2:], 1)
    spot = lax.broadcasted_iota(jnp.int32, ids.shape[2:], 0)
    half = each // 2

    def widen(row):
        one = jnp.broadcast_to(row, (16, 128)).astype(BF16)
        return jnp.concatenate([one] * (CHUNK // 16), axis=0)

    def count(r, p, use=None, start=0):
        pair = jnp.where(lane < each, ids[r, 2 * p], ids[r, 2 * p + 1])
        times = jnp.ones(pair.shape, F32)
        for i in range(bag - 1):
            again = (spot > i) & (pair == pair[i : i + 1])
            times = times + jnp.where(again, 1.0, 0.0)

        def step(q, carry):
            base = jnp.where(q < per_block, own_first, mate_first) + (q % per_block) * CHUNK
            local = pair - base
            local = jnp.where((local >= 0) & (local < CHUNK), local, -1).astype(F32)
            acc = jnp.zeros((CHUNK, 128), BF16)
            for j in range(bag):
                acc = jnp.where(widen(local[j : j + 1]) == row16, widen(times[j : j + 1]), acc)
            at = pl.ds(pl.multiple_of(q * CHUNK, CHUNK), CHUNK)
            ct[r, p, at] = acc
            return carry if use is None else use(acc, at, carry, q)

        return lax.fori_loop(0, 2 * per_block, step, start)

    def counts(r):
        def step(p, carry):
            count(r, p)
            return carry

        lax.fori_loop(0, 2, step, 0)

    pcp = {}

    def give(j, h):
        part = pl.ds(h * half, half)
        pcp[j, h] = send(psend.at[j, part], precv.at[j - 1, part], p_sem.at[j - 1, h], line[j])

    def first_part(acc, at, total, q):
        @pl.when(q == per_block)
        def _():
            for cp in tcp:
                cp.wait()
            hi, lo = split(tab[1])
            thi[rows : 2 * rows] = hi
            tlo[rows : 2 * rows] = lo

        return add_part(acc, at, total, q)

    def add_part(acc, at, total, q):
        return total + dot(acc, thi[at], ((0,), (0,))) + dot(acc, tlo[at], ((0,), (0,)))

    for p in (1, 0):
        for j in ((2, 3) if p else (1,)):
            idz[j].wait()
        if not p:
            idx = send(ids.at[0], ids.at[1], idp_sem.at[0], xn)
            idy = send(ids.at[0], ids.at[2], idp_sem.at[1], yn)
        part = count(0, p, first_part if p else add_part, jnp.zeros((128, tab.shape[2]), F32))
        psend[2 * p] = part[0:each]
        psend[2 * p + 1] = part[each : 2 * each]
        for j in (2 * p, 2 * p + 1):
            if j:
                give(j, 0)
    for j in (2, 3, 1):
        give(j, 1)

    idx.wait()
    idd = send(ids.at[1], ids.at[3], idp_sem.at[2], yn)
    counts(1)

    def cross(x, k):
        xh, xl = split(x)
        return dot(xh, wsp[k]) + (dot(xh, wsp[k + 1]) + dot(xl, wsp[k]))

    def block(r, j, h):
        return back.at[r, pl.ds(j * each + h * half, half)]

    zcp, xcp, ycp, dcp = {}, {}, {}, {}

    def forward(j, h):
        xcp[j, h] = send(block(0, j, h), block(1, j, h), bp_sem.at[0, j, h], xn)
        ycp[j, h] = send(block(0, j, h), block(2, j, h), bp_sem.at[1, j, h], yn)

    def process(h):
        at = slice(h * half, (h + 1) * half)
        for j in (1, 2, 3):
            pcp[j, h].wait()
        pooled = (psend[0, at] + precv[0, at]) + (precv[1, at] + precv[2, at])
        grad = up[at]
        mixed = cross(pooled, 0) + bias[...]
        back[0, at] = grad * mixed + cross(grad * pooled, 2) + grad
        for j in (2, 3, 1) if h else (2, 1):
            zcp[j, h] = send(block(0, 0, h), block(0, j, h), bz_sem.at[j - 1, h], line[j])
        forward(0, h)
        crossed_ref[at] = pooled * mixed + pooled

    def along(j, h):
        zcp[j, h].wait_recv()
        if j == 2 and h == 0:
            zcp[3, h] = send(block(0, 2, h), block(0, 3, h), bz_sem.at[2, h], line[1])
        forward(j, h)

    def diagonal(j, h):
        xcp[j, h].wait_recv()
        ycp[j, h].wait_recv()
        if (j + h) % 2:
            dcp[j, h] = send(block(1, j, h), block(3, j, h), bd_sem.at[j, h], yn)
        else:
            dcp[j, h] = send(block(2, j, h), block(3, j, h), bd_sem.at[j, h], xn)

    process(0)
    idy.wait()
    counts(2)
    along(1, 0)
    diagonal(0, 0)
    process(1)
    stores = [pltpu.make_async_copy(crossed_ref, crossed_out, store_sem.at[0])]
    stores[0].start()
    along(2, 0)
    diagonal(1, 0)
    idd.wait()
    counts(3)
    along(3, 0)
    along(1, 1)
    diagonal(0, 1)
    along(2, 1)
    diagonal(2, 0)
    dcp[0, 1].wait_recv()
    for j in (2, 3, 1):
        dcp[j, 1] = send(block(3, 0, 1), block(3, j, 1), bd_sem.at[j, 1], line[j])
    along(3, 1)
    diagonal(3, 0)
    for j in (1, 2, 3):
        xcp[j, 1].wait_recv()
        ycp[j, 1].wait_recv()

    def product(r, q):
        bh, bl = split(back[r])
        at = pl.ds(pl.multiple_of(q * CHUNK, CHUNK), CHUNK)
        c = jnp.concatenate([ct[r, 0, at], ct[r, 1, at]], axis=1)
        g[r, at] = dot(c, bh) + dot(c, bl)
        return at

    def early(i, carry):
        product(i // (2 * per_block), i % (2 * per_block))
        return carry

    lax.fori_loop(0, (PLANE - 1) * 2 * per_block, early, 0)
    for at, cp in dcp.items():
        if at != (0, 1):
            cp.wait_recv()

    def swap(i):
        return pltpu.make_async_remote_copy(
            src_ref=g.at[0, pl.ds(rows + i * SLAB, SLAB)],
            dst_ref=grecv.at[pl.ds(i * SLAB, SLAB)],
            send_sem=g_sem.at[i, 0], recv_sem=g_sem.at[i, 1],
            device_id=mate, device_id_type=MESH,
        )

    def late(i, carry):
        q = (i + per_block) % (2 * per_block)
        at = product(3, q)
        g[0, at] = (g[0, at] + g[1, at]) + (g[2, at] + g[3, at])

        @pl.when(i < per_block)
        def _():
            for k in range(CHUNK // SLAB):
                swap(i * (CHUNK // SLAB) + k).start()

        return carry

    lax.fori_loop(0, 2 * per_block, late, 0)
    piece = CHUNK
    acc_col = jnp.transpose(jnp.broadcast_to(accum[...], (8, rows)))[:, 0:1]
    for d in (zcp, xcp, ycp, dcp):
        for cp in d.values():
            cp.wait_send()
    for i in range(per_block):
        for k in range(CHUNK // SLAB):
            swap(i * (CHUNK // SLAB) + k).wait()
        at = slice(i * piece, (i + 1) * piece)
        total = g[0, at] + grecv[at]
        mean = jnp.sum(total * total, axis=1, keepdims=True) * (1.0 / total.shape[1])
        fresh = acc_col[at] + mean
        newt_ref[at] = tab[0, at] - 0.5 * total * lax.rsqrt(fresh)
        part = pl.ds(i * piece, piece)
        stores.append(pltpu.make_async_copy(newt_ref.at[part], newt_out.at[part], store_sem.at[1 + i]))
        stores[-1].start()
        newa_ref[:, at] = jnp.transpose(jnp.broadcast_to(fresh, (piece, 128)))[0:1]
    stores.append(pltpu.make_async_copy(newa_ref, newa_out, store_sem.at[1 + per_block]))
    stores[-1].start()
    for cp in stores:
        cp.wait()


def hand_out(a, b, c, x, y, w, va, vb, vc, sems_in, sems_out):
    piece = vb.shape[0] // 2
    parts = [(b.at[pl.ds(i * piece, piece)], vb.at[pl.ds(i * piece, piece)], y.at[pl.ds(i * piece, piece)]) for i in (0, 1)]
    parts += [(a, va, x), (c, vc, w)]
    ins = [pltpu.make_async_copy(p[0], p[1], sems_in.at[i]) for i, p in enumerate(parts)]
    outs = [pltpu.make_async_copy(p[1], p[2], sems_out.at[i]) for i, p in enumerate(parts)]
    for cp in ins:
        cp.start()
    for cp, out in zip(ins, outs):
        cp.wait()
        out.start()
    for cp in outs:
        cp.wait()


def fused_body(bag_ids, table, accum, cross_weight, cross_bias, upstream):
    each, bag = bag_ids.shape
    rows, width = table.shape
    tall = -(-bag // 8) * 8
    hbm = pl.BlockSpec(memory_space=pltpu.HBM)
    dma = pltpu.SemaphoreType.DMA
    shapes = (
        jax.ShapeDtypeStruct((each, width), F32),
        jax.ShapeDtypeStruct((rows, width), F32),
        jax.ShapeDtypeStruct((1, rows), F32),
    )
    done = pl.pallas_call(
        lambda *refs: kernel(bag, *refs),
        out_shape=shapes,
        in_specs=[hbm] * 6,
        out_specs=[hbm] * 3,
        scratch_shapes=[
            pltpu.VMEM((2, rows, width), F32),
            pltpu.VMEM((2 * rows, width), BF16),
            pltpu.VMEM((2 * rows, width), BF16),
            pltpu.VMEM((PLANE, LINE, tall, 128), jnp.int32),
            pltpu.VMEM((PLANE, 2, 2 * rows, 2 * each), BF16),
            pltpu.VMEM((LINE, each, width), F32),
            pltpu.VMEM((LINE - 1, each, width), F32),
            pltpu.VMEM((PLANE, LINE * each, width), F32),
            pltpu.VMEM((PLANE, 2 * rows, width), F32),
            pltpu.VMEM((rows, width), F32),
            pltpu.VMEM((bag, each), jnp.int32),
            pltpu.VMEM((1, rows), F32),
            pltpu.VMEM((width, width), F32),
            pltpu.VMEM((1, width), F32),
            pltpu.VMEM((each, width), F32),
            pltpu.VMEM((4, width, width), BF16),
            pltpu.VMEM((each, width), F32),
            pltpu.VMEM((rows, width), F32),
            pltpu.VMEM((1, rows), F32),
            dma((6,)),
            dma((2 + rows // CHUNK,)),
            dma((rows // SLAB, 2)),
            dma((3, 2)),
            dma((3, 2)),
            dma((3, 2, 2)),
            dma((3, 2, 2)),
            dma((2, LINE, 2, 2)),
            dma((LINE, 2, 2)),
            dma((rows // SLAB, 2)),
        ],
        compiler_params=pltpu.CompilerParams(
            collective_id=0, has_side_effects=True, vmem_limit_bytes=GRANT
        ),
    )(bag_ids.T, table, accum.reshape(1, rows), cross_weight, cross_bias.reshape(1, width), upstream)
    crossed, new_table, new_accum = pl.pallas_call(
        hand_out,
        out_shape=shapes,
        in_specs=[hbm] * 3,
        out_specs=[hbm] * 3,
        scratch_shapes=[pltpu.VMEM(a.shape, F32) for a in shapes] + [dma((4,)), dma((4,))],
        compiler_params=pltpu.CompilerParams(vmem_limit_bytes=GRANT),
    )(*done)
    return crossed, new_table, new_accum.reshape(rows)


def adagrad_rows(rows, sums, grads):
    fresh = sums + jnp.mean(grads * grads, axis=1)
    return (rows - 0.5 * grads / jnp.sqrt(fresh)[:, None], fresh)


def general_body(bag_ids, table, accum, cross_weight, cross_bias, upstream):
    rows_owned = table.shape[0]
    first_row = lax.axis_index("shard") * rows_owned
    group_ids = lax.all_gather(bag_ids, "shard", axis=0, tiled=True)
    local = group_ids - first_row
    number = lax.broadcasted_iota(jnp.int32, (1, rows_owned), 1)
    counts = jnp.zeros((local.shape[0], rows_owned), F32)
    for j in range(local.shape[1]):
        counts = counts + (local[:, j : j + 1] == number).astype(F32)
    pooled = lax.psum_scatter(
        jnp.dot(counts, table, precision=lax.Precision.HIGHEST),
        "shard",
        scatter_dimension=0,
        tiled=True,
    )
    mixed = jnp.dot(pooled, cross_weight, precision=lax.Precision.HIGHEST) + cross_bias
    crossed = pooled * mixed + pooled
    back = (
        upstream * mixed
        + jnp.dot(upstream * pooled, cross_weight.T, precision=lax.Precision.HIGHEST)
        + upstream
    )
    piece = lax.all_gather(back, "shard", axis=0, tiled=True)
    added = lax.dot_general(
        counts, piece, (((0,), (0,)), ((), ())), precision=lax.Precision.HIGHEST
    )
    totals = lax.psum(added, "rep")
    new_table, new_accum = adagrad_rows(table, accum, totals)
    return (crossed, new_table, new_accum)


def solution(mesh):
    placed = (
        P(("rep", "shard"), None),
        P("shard", None),
        P("shard"),
        P(),
        P(),
        P(("rep", "shard"), None),
    )
    small = mesh.shape["rep"] == PLANE and mesh.shape["shard"] == 2 * LINE
    return jax.shard_map(
        fused_body if small else general_body,
        mesh=mesh,
        in_specs=placed,
        out_specs=(P(("rep", "shard"), None), P("shard", None), P("shard")),
        check_vma=False,
    )
```

```python
import jax
import jax.numpy as jnp
from jax import lax
from jax.experimental import pallas as pl
from jax.experimental.pallas import tpu as pltpu
from jax.sharding import PartitionSpec as P

F32 = jnp.float32
BF16 = jnp.bfloat16
MESH = pl.DeviceIdType.MESH
PLANE = 4
LINE = 4
GRANT = 63 * 1024 * 1024
CHUNK = 256


def split(x):
    hi = x.astype(BF16)
    return hi, (x - hi.astype(F32)).astype(BF16)


def dot(a, b, dims=((1,), (0,))):
    return lax.dot_general(a, b, (dims, ((), ())), preferred_element_type=F32)


def kernel(
    bag, ids_hbm, table_hbm, accum_hbm, weight_hbm, bias_hbm, up_hbm,
    crossed_out, newt_out, newa_out,
    tab, thi, tlo, ids, ct, psend, precv, back, g, grecv,
    ids_raw, accum, weight, bias, up, wsp, crossed_ref, newt_ref, newa_ref,
    load_sem, store_sem, tab_sem, idz_sem, idp_sem, p_sem, bz_sem, bp_sem, bd_sem, g_sem,
):
    rep = lax.axis_index("rep")
    shard = lax.axis_index("shard")
    z = shard // 2
    core = shard % 2
    rows = tab.shape[1]
    each = up.shape[0]
    mate = (rep, shard + 1 - 2 * core)
    xn = (rep + 1 - 2 * (rep % 2), shard)
    yn = ((rep + 2) % 4, shard)
    dn = (PLANE - 1 - rep, shard)
    line = {
        1: (rep, (z + 1 - 2 * (z % 2)) * 2 + core),
        2: (rep, ((z + 2) % LINE) * 2 + core),
        3: (rep, (LINE - 1 - z) * 2 + core),
    }

    def send(src, dst, sems, to):
        cp = pltpu.make_async_remote_copy(
            src_ref=src, dst_ref=dst, send_sem=sems.at[0], recv_sem=sems.at[1],
            device_id=to, device_id_type=MESH,
        )
        cp.start()
        return cp

    barrier = pltpu.get_barrier_semaphore()
    for to in (mate, xn, yn, dn, line[1], line[2], line[3]):
        pl.semaphore_signal(barrier, inc=1, device_id=to, device_id_type=MESH)

    def load(src, dst, i):
        cp = pltpu.make_async_copy(src, dst, load_sem.at[i])
        cp.start()
        return cp

    ids_load = load(ids_hbm, ids_raw, 0)
    table_load = load(table_hbm, tab.at[0], 1)
    rest = [
        load(src, dst, 2 + i)
        for i, (src, dst) in enumerate(
            ((weight_hbm, weight), (up_hbm, up), (bias_hbm, bias), (accum_hbm, accum))
        )
    ]
    ids_load.wait()
    raw = ids_raw[...]
    ids[0, 0] = jnp.full(ids.shape[2:], -1, jnp.int32)
    ids[0, 0, 0:bag] = jnp.concatenate([raw, raw], axis=1)
    pl.semaphore_wait(barrier, 7)

    idz = {j: send(ids.at[0, 0], ids.at[0, j], idz_sem.at[j - 1], line[j]) for j in (2, 3, 1)}
    tcp = send(table_hbm, tab.at[1], tab_sem, mate)
    table_load.wait()
    hi, lo = split(tab[0])
    thi[0:rows] = hi
    tlo[0:rows] = lo

    for cp in rest:
        cp.wait()
    hi, lo = split(weight[...])
    wsp[0] = hi
    wsp[1] = lo
    turned = jnp.transpose(weight[...])
    hi, lo = split(turned)
    wsp[2] = hi
    wsp[3] = lo

    own_first = shard * rows
    mate_first = (shard + 1 - 2 * core) * rows
    per_block = rows // CHUNK
    row16 = lax.broadcasted_iota(jnp.int32, (CHUNK, 128), 0).astype(F32).astype(BF16)
    lane = lax.broadcasted_iota(jnp.int32, ids.shape[2:], 1)
    spot = lax.broadcasted_iota(jnp.int32, ids.shape[2:], 0)
    half = each // 2

    def widen(row):
        one = jnp.broadcast_to(row, (16, 128)).astype(BF16)
        return jnp.concatenate([one] * (CHUNK // 16), axis=0)

    def count(r, p, use=None, start=0):
        pair = jnp.where(lane < each, ids[r, 2 * p], ids[r, 2 * p + 1])
        times = jnp.ones(pair.shape, F32)
        for i in range(bag - 1):
            again = (spot > i) & (pair == pair[i : i + 1])
            times = times + jnp.where(again, 1.0, 0.0)

        def step(q, carry):
            base = jnp.where(q < per_block, own_first, mate_first) + (q % per_block) * CHUNK
            local = pair - base
            local = jnp.where((local >= 0) & (local < CHUNK), local, -1).astype(F32)
            acc = jnp.zeros((CHUNK, 128), BF16)
            for j in range(bag):
                acc = jnp.where(widen(local[j : j + 1]) == row16, widen(times[j : j + 1]), acc)
            at = pl.ds(pl.multiple_of(q * CHUNK, CHUNK), CHUNK)
            ct[r, p, at] = acc
            return carry if use is None else use(acc, at, carry)

        return lax.fori_loop(0, 2 * per_block, step, start)

    def counts(r):
        def step(p, carry):
            count(r, p)
            return carry

        lax.fori_loop(0, 2, step, 0)

    pcp = {}

    def give(j, h):
        part = pl.ds(h * half, half)
        pcp[j, h] = send(psend.at[j, part], precv.at[j - 1, part], p_sem.at[j - 1, h], line[j])

    def add_part(acc, at, total):
        return total + dot(acc, thi[at], ((0,), (0,))) + dot(acc, tlo[at], ((0,), (0,)))

    for p in (1, 0):
        for j in ((2, 3) if p else (1,)):
            idz[j].wait()
        if p:
            tcp.wait()
            hi, lo = split(tab[1])
            thi[rows : 2 * rows] = hi
            tlo[rows : 2 * rows] = lo
        else:
            idx = send(ids.at[0], ids.at[1], idp_sem.at[0], xn)
            idy = send(ids.at[0], ids.at[2], idp_sem.at[1], yn)
        part = count(0, p, add_part, jnp.zeros((128, tab.shape[2]), F32))
        psend[2 * p] = part[0:each]
        psend[2 * p + 1] = part[each : 2 * each]
        for j in (2 * p, 2 * p + 1):
            if j:
                give(j, 0)
    for j in (2, 3, 1):
        give(j, 1)

    idx.wait()
    idd = send(ids.at[1], ids.at[3], idp_sem.at[2], yn)
    counts(1)

    def cross(x, k):
        xh, xl = split(x)
        return dot(xh, wsp[k]) + (dot(xh, wsp[k + 1]) + dot(xl, wsp[k]))

    def block(r, j, h):
        return back.at[r, pl.ds(j * each + h * half, half)]

    zcp, xcp, ycp, dcp = {}, {}, {}, {}

    def forward(j, h):
        xcp[j, h] = send(block(0, j, h), block(1, j, h), bp_sem.at[0, j, h], xn)
        ycp[j, h] = send(block(0, j, h), block(2, j, h), bp_sem.at[1, j, h], yn)

    def process(h):
        at = slice(h * half, (h + 1) * half)
        for j in (1, 2, 3):
            pcp[j, h].wait()
        pooled = (psend[0, at] + precv[0, at]) + (precv[1, at] + precv[2, at])
        grad = up[at]
        mixed = cross(pooled, 0) + bias[...]
        back[0, at] = grad * mixed + cross(grad * pooled, 2) + grad
        for j in (2, 3, 1) if h else (2, 1):
            zcp[j, h] = send(block(0, 0, h), block(0, j, h), bz_sem.at[j - 1, h], line[j])
        forward(0, h)
        crossed_ref[at] = pooled * mixed + pooled

    def along(j, h):
        zcp[j, h].wait_recv()
        if j == 2 and h == 0:
            zcp[3, h] = send(block(0, 2, h), block(0, 3, h), bz_sem.at[2, h], line[1])
        forward(j, h)
        if h and j > 1:
            dcp[j, h] = send(block(0, j, h), block(3, j, h), bd_sem.at[j, h], dn)

    def diagonal(j, h):
        xcp[j, h].wait_recv()
        ycp[j, h].wait_recv()
        if (j + h) % 2:
            dcp[j, h] = send(block(1, j, h), block(3, j, h), bd_sem.at[j, h], yn)
        else:
            dcp[j, h] = send(block(2, j, h), block(3, j, h), bd_sem.at[j, h], xn)

    process(0)
    idy.wait()
    counts(2)
    along(1, 0)
    diagonal(0, 0)
    process(1)
    stores = [pltpu.make_async_copy(crossed_ref, crossed_out, store_sem.at[0])]
    stores[0].start()
    along(2, 0)
    diagonal(1, 0)
    idd.wait()
    counts(3)
    along(3, 0)
    along(1, 1)
    diagonal(0, 1)
    along(2, 1)
    diagonal(2, 0)
    along(3, 1)
    diagonal(1, 1)
    diagonal(3, 0)

    def product(r, q):
        bh, bl = split(back[r])
        at = pl.ds(pl.multiple_of(q * CHUNK, CHUNK), CHUNK)
        c = jnp.concatenate([ct[r, 0, at], ct[r, 1, at]], axis=1)
        g[r, at] = dot(c, bh) + dot(c, bl)
        return at

    def whole(r):
        bh, bl = split(back[r])
        c = jnp.concatenate([ct[r, 0], ct[r, 1]], axis=1)
        g[r] = dot(c, bh) + dot(c, bl)

    whole(0)
    for j in (2, 3):
        xcp[j, 1].wait_recv()
    whole(1)
    for j in (2, 3):
        ycp[j, 1].wait_recv()
    whole(2)
    for cp in dcp.values():
        cp.wait_recv()

    def swap(i):
        return pltpu.make_async_remote_copy(
            src_ref=g.at[0, pl.ds(rows + i * CHUNK, CHUNK)],
            dst_ref=grecv.at[pl.ds(i * CHUNK, CHUNK)],
            send_sem=g_sem.at[i, 0], recv_sem=g_sem.at[i, 1],
            device_id=mate, device_id_type=MESH,
        )

    def late(i, carry):
        q = (i + per_block) % (2 * per_block)
        at = product(3, q)
        g[0, at] = (g[0, at] + g[1, at]) + (g[2, at] + g[3, at])

        @pl.when(i < per_block)
        def _():
            swap(i).start()

        return carry

    lax.fori_loop(0, 2 * per_block, late, 0)
    piece = CHUNK
    acc_col = jnp.transpose(jnp.broadcast_to(accum[...], (8, rows)))[:, 0:1]
    for d in (zcp, xcp, ycp, dcp):
        for cp in d.values():
            cp.wait_send()
    for i in range(per_block):
        swap(i).wait()
        at = slice(i * piece, (i + 1) * piece)
        total = g[0, at] + grecv[at]
        mean = jnp.sum(total * total, axis=1, keepdims=True) * (1.0 / total.shape[1])
        fresh = acc_col[at] + mean
        newt_ref[at] = tab[0, at] - 0.5 * total * lax.rsqrt(fresh)
        part = pl.ds(i * piece, piece)
        stores.append(pltpu.make_async_copy(newt_ref.at[part], newt_out.at[part], store_sem.at[1 + i]))
        stores[-1].start()
        newa_ref[:, at] = jnp.transpose(jnp.broadcast_to(fresh, (piece, 128)))[0:1]
    stores.append(pltpu.make_async_copy(newa_ref, newa_out, store_sem.at[1 + per_block]))
    stores[-1].start()
    for cp in stores:
        cp.wait()


def hand_out(a, b, c, x, y, w, va, vb, vc, sems_in, sems_out):
    piece = vb.shape[0] // 2
    parts = [(b.at[pl.ds(i * piece, piece)], vb.at[pl.ds(i * piece, piece)], y.at[pl.ds(i * piece, piece)]) for i in (0, 1)]
    parts += [(a, va, x), (c, vc, w)]
    ins = [pltpu.make_async_copy(p[0], p[1], sems_in.at[i]) for i, p in enumerate(parts)]
    outs = [pltpu.make_async_copy(p[1], p[2], sems_out.at[i]) for i, p in enumerate(parts)]
    for cp in ins:
        cp.start()
    for cp, out in zip(ins, outs):
        cp.wait()
        out.start()
    for cp in outs:
        cp.wait()


def fused_body(bag_ids, table, accum, cross_weight, cross_bias, upstream):
    each, bag = bag_ids.shape
    rows, width = table.shape
    tall = -(-bag // 8) * 8
    hbm = pl.BlockSpec(memory_space=pltpu.HBM)
    dma = pltpu.SemaphoreType.DMA
    shapes = (
        jax.ShapeDtypeStruct((each, width), F32),
        jax.ShapeDtypeStruct((rows, width), F32),
        jax.ShapeDtypeStruct((1, rows), F32),
    )
    done = pl.pallas_call(
        lambda *refs: kernel(bag, *refs),
        out_shape=shapes,
        in_specs=[hbm] * 6,
        out_specs=[hbm] * 3,
        scratch_shapes=[
            pltpu.VMEM((2, rows, width), F32),
            pltpu.VMEM((2 * rows, width), BF16),
            pltpu.VMEM((2 * rows, width), BF16),
            pltpu.VMEM((PLANE, LINE, tall, 128), jnp.int32),
            pltpu.VMEM((PLANE, 2, 2 * rows, 2 * each), BF16),
            pltpu.VMEM((LINE, each, width), F32),
            pltpu.VMEM((LINE - 1, each, width), F32),
            pltpu.VMEM((PLANE, LINE * each, width), F32),
            pltpu.VMEM((PLANE, 2 * rows, width), F32),
            pltpu.VMEM((rows, width), F32),
            pltpu.VMEM((bag, each), jnp.int32),
            pltpu.VMEM((1, rows), F32),
            pltpu.VMEM((width, width), F32),
            pltpu.VMEM((1, width), F32),
            pltpu.VMEM((each, width), F32),
            pltpu.VMEM((4, width, width), BF16),
            pltpu.VMEM((each, width), F32),
            pltpu.VMEM((rows, width), F32),
            pltpu.VMEM((1, rows), F32),
            dma((6,)),
            dma((2 + rows // CHUNK,)),
            dma((2,)),
            dma((3, 2)),
            dma((3, 2)),
            dma((3, 2, 2)),
            dma((3, 2, 2)),
            dma((2, LINE, 2, 2)),
            dma((LINE, 2, 2)),
            dma((rows // CHUNK, 2)),
        ],
        compiler_params=pltpu.CompilerParams(
            collective_id=0, has_side_effects=True, vmem_limit_bytes=GRANT
        ),
    )(bag_ids.T, table, accum.reshape(1, rows), cross_weight, cross_bias.reshape(1, width), upstream)
    crossed, new_table, new_accum = pl.pallas_call(
        hand_out,
        out_shape=shapes,
        in_specs=[hbm] * 3,
        out_specs=[hbm] * 3,
        scratch_shapes=[pltpu.VMEM(a.shape, F32) for a in shapes] + [dma((4,)), dma((4,))],
        compiler_params=pltpu.CompilerParams(vmem_limit_bytes=GRANT),
    )(*done)
    return crossed, new_table, new_accum.reshape(rows)


def adagrad_rows(rows, sums, grads):
    fresh = sums + jnp.mean(grads * grads, axis=1)
    return (rows - 0.5 * grads / jnp.sqrt(fresh)[:, None], fresh)


def general_body(bag_ids, table, accum, cross_weight, cross_bias, upstream):
    rows_owned = table.shape[0]
    first_row = lax.axis_index("shard") * rows_owned
    group_ids = lax.all_gather(bag_ids, "shard", axis=0, tiled=True)
    local = group_ids - first_row
    number = lax.broadcasted_iota(jnp.int32, (1, rows_owned), 1)
    counts = jnp.zeros((local.shape[0], rows_owned), F32)
    for j in range(local.shape[1]):
        counts = counts + (local[:, j : j + 1] == number).astype(F32)
    pooled = lax.psum_scatter(
        jnp.dot(counts, table, precision=lax.Precision.HIGHEST),
        "shard",
        scatter_dimension=0,
        tiled=True,
    )
    mixed = jnp.dot(pooled, cross_weight, precision=lax.Precision.HIGHEST) + cross_bias
    crossed = pooled * mixed + pooled
    back = (
        upstream * mixed
        + jnp.dot(upstream * pooled, cross_weight.T, precision=lax.Precision.HIGHEST)
        + upstream
    )
    piece = lax.all_gather(back, "shard", axis=0, tiled=True)
    added = lax.dot_general(
        counts, piece, (((0,), (0,)), ((), ())), precision=lax.Precision.HIGHEST
    )
    totals = lax.psum(added, "rep")
    new_table, new_accum = adagrad_rows(table, accum, totals)
    return (crossed, new_table, new_accum)


def solution(mesh):
    placed = (
        P(("rep", "shard"), None),
        P("shard", None),
        P("shard"),
        P(),
        P(),
        P(("rep", "shard"), None),
    )
    small = mesh.shape["rep"] == PLANE and mesh.shape["shard"] == 2 * LINE
    return jax.shard_map(
        fused_body if small else general_body,
        mesh=mesh,
        in_specs=placed,
        out_specs=(P(("rep", "shard"), None), P("shard", None), P("shard")),
        check_vma=False,
    )
```
